256 devices in a mesh: freq: 2 (over core), inl: 16 (over y, x), xl: 8 (over z).
Axes of the slice: x: 4, y: 4, z: 8, core: 2. Of those that a mesh axis runs over, the one named last changes fastest.
Arguments:
- spectra: float32 [2, 2, 256, 1024], P('freq', None, 'inl', 'xl'), parts along dimension 0, may hold values from -6 to 6
- omega: float32 [2, 289, 64], replicated, may hold values from -0.25 to 0.25
Outputs:
- sketch: float32 [2, 128, 256, 1024], P('freq', None, 'inl', 'xl'), parts along dimension 0
- denoised: float32 [2, 2, 256, 1024], P('freq', None, 'inl', 'xl'), parts along dimension 0
The draws below stay inside these ranges and needn't reach their ends.
There are 2 independent parts, one for each index of `freq`. The reference program is written for one: setup_inputs(seed, part) draws one part's arguments, and reference() takes and returns one part's arrays. A program takes and returns all parts, laid end to end along the dimension named above; an argument that names none is the same for every part. Nothing has to cross between parts.
All inputs are finite; a program needn't handle non-finite values.
Results may differ from the reference program's by a relative error of at most 0.0001.
Values sent between devices are 32-bit elements; how exact they have to be, the bound alone decides.
A program may use at most 64 MiB of HBM per device.

```python
import jax
import jax.numpy as jnp
from jax import lax

KI = 17
RANK = 64
FQ = 1
HW = 8
TAPS = 289
NI = 256
NX = 1024


def block_scale(stream_key, dims, cuts, smallest, high):
    def one(dim, shards_of):
        draws = jax.random.uniform(jax.random.fold_in(jax.random.fold_in(stream_key, 6), dim), (shards_of,), jnp.float32, smallest / len(cuts), high / len(cuts))
        return jnp.repeat(jnp.exp(draws), dims[dim] // shards_of).reshape((-1,) + (1,) * (len(dims) - dim - 1))

    gain = one(*cuts[0])
    for cut in cuts[1:]:
        gain = gain * one(*cut)
    return gain


def normal_values(own_key, extent, scale, reach, cuts=(), held_as=jnp.bfloat16):
    array = jax.random.normal(own_key, extent, jnp.float32) * scale
    if len(cuts) > 0:
        array = block_scale(own_key, extent, cuts, -0.22, 0.18) * array
    return jnp.clip(array, min=-reach, max=reach).astype(held_as)


def setup_inputs(seed: int = 0, part: int = 0) -> dict:
    streams_of = jax.random.split(jax.random.key(seed), 3)
    part_splits = jax.random.split(jax.random.fold_in(streams_of[2], part), 3)
    return {
        "spectra": normal_values(part_splits[0], (FQ, 2, NI, NX), 1.0, 6.0, ((2, 16), (3, 8)), jnp.float32),
        "omega": normal_values(streams_of[1], (2, TAPS, RANK), (2 * TAPS) ** -0.5, 0.25, (), jnp.float32),
    }


PRECISE = lax.Precision.HIGHEST

def sketch_weights(omega):
    from_real = jnp.concatenate([omega[0], omega[1]], axis=1)
    from_imag = jnp.concatenate([-omega[1], omega[0]], axis=1)
    stacked = jnp.stack([from_real, from_imag], axis=1)
    return stacked.reshape(KI, KI * 2, stacked.shape[2])

def tap_patches(padded, shift_row, rows, cols):
    pieces = [padded[:, :, shift_row:shift_row + rows, shift_col:shift_col + cols] for shift_col in range(KI)]
    return jnp.stack(pieces, axis=1)

def correlate(padded, weights, rows, cols):
    result = None
    for shift_row in range(KI):
        patches = tap_patches(padded, shift_row, rows, cols)
        flat = patches.reshape(patches.shape[0], KI * 2, rows, cols)
        addend = jnp.einsum('kc,fkab->fcab', weights[shift_row], flat, precision=PRECISE)
        result = addend if result is None else result + addend
    return result

def gram_of(sketch):
    half_rank = sketch.shape[1] // 2
    inner = jnp.einsum('fcab,fdab->fcd', sketch, sketch, precision=PRECISE)
    real_real = inner[:, :half_rank, :half_rank]
    real_imag = inner[:, :half_rank, half_rank:]
    imag_real = inner[:, half_rank:, :half_rank]
    imag_imag = inner[:, half_rank:, half_rank:]
    upper_rows = jnp.concatenate([real_real + imag_imag, imag_real - real_imag], axis=2)
    lower_rows = jnp.concatenate([real_imag - imag_real, imag_imag + real_real], axis=2)
    return jnp.concatenate([upper_rows, lower_rows], axis=1)

def moments_of(sketch, padded, rows, cols):
    half_rank = sketch.shape[1] // 2
    columns = []
    for shift_row in range(KI):
        patches = tap_patches(padded, shift_row, rows, cols)
        product = jnp.einsum('fcab,fqxab->fcqx', sketch, patches, precision=PRECISE)
        top = product[:, :half_rank, :, 0] + product[:, half_rank:, :, 1]
        bottom = product[:, :half_rank, :, 1] - product[:, half_rank:, :, 0]
        columns.append(jnp.concatenate([top, bottom], axis=1))
    return jnp.concatenate(columns, axis=2)

def solve_both(lower, moments):
    middle = lax.linalg.triangular_solve(lower, moments, left_side=True, lower=True)
    return lax.linalg.triangular_solve(lower, middle, left_side=True, lower=True, transpose_a=True)

def tap_mixer(coeffs, shift_row):
    half_rank = coeffs.shape[1] // 2
    block = coeffs[:, :, shift_row * KI:(shift_row + 1) * KI]
    top = block[:, :half_rank]
    bottom = block[:, half_rank:]
    real_out = jnp.concatenate([top, -bottom], axis=1)
    imag_out = jnp.concatenate([bottom, top], axis=1)
    return jnp.stack([real_out, imag_out], axis=3)

def spread(sketch, coeffs, rows, cols):
    extended = jnp.zeros((sketch.shape[0], 2, rows + 2 * HW, cols + 2 * HW), jnp.float32)
    for shift_row in range(KI):
        values = jnp.einsum('fcqx,fcab->fqxab', tap_mixer(coeffs, shift_row), sketch, precision=PRECISE)
        for shift_col in range(KI):
            extended = extended.at[:, :, shift_row:shift_row + rows, shift_col:shift_col + cols].add(values[:, shift_col])
    return extended

def coverage(start, length, total):
    index = start + jnp.arange(length, dtype=jnp.int32)
    return (jnp.minimum(index + HW, total - 1) - jnp.maximum(index - HW, 0) + 1).astype(jnp.float32)

def reference(spectra, omega):
    weights = sketch_weights(omega)
    counts = coverage(0, NI, NI)[:, None] * coverage(0, NX, NX)[None, :]
    sketches = []
    outputs = []
    for index in range(FQ):
        data = spectra[index:index + 1]
        padded = jnp.pad(data, ((0, 0), (0, 0), (HW, HW), (HW, HW)))
        sketch = correlate(padded, weights, NI, NX)
        gram = gram_of(sketch)
        moments = moments_of(sketch, padded, NI, NX)
        lower = jnp.linalg.cholesky(gram)
        coeffs = solve_both(lower, moments)
        extended = spread(sketch, coeffs, NI, NX)
        outputs.append(extended[:, :, HW:HW + NI, HW:HW + NX] / counts)
        sketches.append(sketch)
    return (jnp.concatenate(sketches, axis=0), jnp.concatenate(outputs, axis=0))
```

```python
import functools

import jax
import jax.numpy as jnp
from jax import lax
from jax.experimental import pallas as pl
from jax.experimental.pallas import tpu as pltpu
from jax.sharding import PartitionSpec as P

MESH = pl.DeviceIdType.MESH
F32 = jnp.float32
BF16 = jnp.bfloat16
KI = 17
HW = 8
WIN = 24
GROUPS = 2 * KI
KROWS = GROUPS * WIN
KPAD = 896
TROWS = 384
LANES = 128
CH = 128
HALF = 64


def split(value):
    high = value.astype(BF16)
    return high, (value - high.astype(F32)).astype(BF16)


def mm(a, b):
    return jnp.dot(a, b, preferred_element_type=F32)


def mm_exact(a, b):
    return jnp.dot(a, b, preferred_element_type=F32, precision=lax.Precision.HIGHEST)


def mm_t(a, b):
    return lax.dot_general(a, b, (((1,), (1,)), ((), ())), preferred_element_type=F32)


def roll(value, amount, axis=1):
    size = value.shape[axis]
    amount = amount % size
    return value if amount == 0 else pltpu.roll(value, amount, axis)


def lane_iota(rows, lanes=LANES):
    return lax.broadcasted_iota(jnp.int32, (rows, lanes), 1)


def prepare_weights(omega_ref, taps_ref, compact_ref, band_hi, band_lo):
    taps_ref[...] = jnp.zeros_like(taps_ref)
    taps_ref[0 : KI * KI, :] = jnp.concatenate([omega_ref[0], omega_ref[1]], axis=1)
    taps = taps_ref[...]
    tap_t = taps.T
    turned = jnp.concatenate([-tap_t[HALF:], tap_t[:HALF]], axis=0)
    col = lane_iota(1, KPAD)
    second = col >= KROWS // 2
    inner = jnp.where(second, col - KROWS // 2, col)
    q = (inner * 2731) >> 16
    r = inner - q * WIN
    tap = jnp.where((r < KI) & (col < KROWS), r * KI + q, -1)
    row = lax.broadcasted_iota(jnp.int32, (TROWS, KPAD), 0)
    pick_re = (row == jnp.where(second, -1, tap)).astype(F32).astype(BF16)
    pick_im = (row == jnp.where(second, tap, -1)).astype(F32).astype(BF16)
    re_hi, re_lo = split(tap_t)
    im_hi, im_lo = split(turned)
    wide_hi = mm(re_hi, pick_re) + mm(im_hi, pick_im)
    wide_lo = mm(re_lo, pick_re) + mm(im_lo, pick_im)
    for shift in range(8):
        band_hi[shift * CH : (shift + 1) * CH, :] = roll(wide_hi, shift).astype(BF16)
        band_lo[shift * CH : (shift + 1) * CH, :] = roll(wide_lo, shift).astype(BF16)
    m = lax.broadcasted_iota(jnp.int32, (TROWS, TROWS), 0)
    tap = jnp.where(m < 272, (m & 15) * KI + (m >> 4), jnp.where(m < 289, 16 * KI + m - 272, -1))
    pick = (lane_iota(TROWS, TROWS) == tap).astype(F32)
    compact_ref[...] = mm_exact(pick, taps)


def shifted(left, centre, right, s, lane):
    if s == 0:
        return centre
    if s < 0:
        return jnp.where(lane < -s, roll(left, -s), roll(centre, -s))
    return jnp.where(lane >= LANES - s, roll(right, LANES - s), roll(centre, LANES - s))


def plane(block_ref, x, dc):
    return jnp.concatenate([block_ref[dr, dc, x] for dr in range(3)], axis=0)


def build_main(block_ref, s_hi, s_lo):
    lane = lane_iota(48)
    windows = []
    for x in range(2):
        left, centre, right = (plane(block_ref, x, dc) for dc in range(3))
        for q in range(KI):
            windows.append(shifted(left, centre, right, q - HW, lane))
    for k in range(KI):
        first, second = windows[2 * k], windows[2 * k + 1]
        for g in range(4):
            value = jnp.concatenate([first[8 * g : 8 * g + WIN], second[8 * g : 8 * g + WIN]], axis=0)
            high, low = split(value)
            s_hi[48 * k : 48 * k + 48, g * LANES : (g + 1) * LANES] = high
            s_lo[48 * k : 48 * k + 48, g * LANES : (g + 1) * LANES] = low


def build_side(block_ref, s_hi, s_lo):
    lane = lane_iota(48)
    strips = []
    for x in range(2):
        left, centre, right = (plane(block_ref, x, dc) for dc in range(3))
        for q in range(KI):
            inner = roll(centre, 16 - q)
            near = lane < 16 - q
            strip = jnp.where(
                lane < 8,
                jnp.where(near, roll(left, 16 - q), inner),
                jnp.where(near, inner, roll(right, 16 - q)),
            )
            strip = jnp.where(lane < 16, strip, 0.0)
            total = strip[0:WIN]
            for g in range(1, 4):
                total = total + roll(strip[8 * g : 8 * g + WIN], 16 * g)
            strips.append(total)
    for k in range(KI):
        high, low = split(jnp.concatenate([strips[2 * k], strips[2 * k + 1]], axis=0))
        s_hi[48 * k : 48 * k + 48, 512:640] = high
        s_lo[48 * k : 48 * k + 48, 512:640] = low


def invert(t):
    lane = lane_iota(HALF)
    sub = lax.broadcasted_iota(jnp.int32, (HALF, LANES), 0)
    lane_row = lane_iota(1)
    for k in range(HALF):
        pivot = 1.0 / t[k : k + 1, k : k + 1]
        row = t[k : k + 1, :]
        row = jnp.where(lane_row == k, 1.0, jnp.where(lane_row == HALF + k, 0.0, row)) * pivot
        other = jnp.where(lane_row < HALF, -roll(row, HALF), roll(row, HALF))
        here = sub == k
        real = jnp.where(here, -1.0, t[:, k : k + 1])
        imag = jnp.where(here, 0.0, t[:, HALF + k : HALF + k + 1])
        kept = jnp.where(here | (lane == k) | (lane == HALF + k), 0.0, t)
        t = kept - real * row - imag * other
    return t


def counts(start, length, total, index):
    at = start + index
    return (jnp.minimum(at + HW, total - 1) - jnp.maximum(at - HW, 0) + 1).astype(F32)


def kernel(
    n_inl,
    n_xl,
    spectra_ref,
    omega_ref,
    sketch_out,
    denoised_ref,
    block_ref,
    taps_ref,
    compact_ref,
    band_hi,
    band_lo,
    s_hi,
    s_lo,
    y_hi,
    y_lo,
    sketch_ref,
    prod_ref,
    send_ref,
    recv_a,
    part_ref,
    recv_b,
    full_ref,
    recv_c,
    spread_ref,
    c_hi,
    c_lo,
    halo_send,
    halo_recv,
    a_send,
    a_recv,
    b_send,
    b_recv,
    c_send,
    c_recv,
    out_sem,
):
    inl = lax.axis_index("inl")
    xl = lax.axis_index("xl")
    share = TROWS // n_inl

    up, down = inl > 0, inl < n_inl - 1
    west, east = xl > 0, xl < n_xl - 1
    barrier = pltpu.get_barrier_semaphore()
    sides = [(dr, dc) for dr in (-1, 0, 1) for dc in (-1, 0, 1) if (dr, dc) != (0, 0)]

    def exists(dr, dc):
        ok = None
        for step, low, high in ((dr, up, down), (dc, west, east)):
            if step != 0:
                one = low if step < 0 else high
                ok = one if ok is None else ok & one
        return ok

    for k in range(1, n_inl):
        pl.semaphore_signal(
            barrier, inc=1, device_id={"inl": lax.rem(inl + k, n_inl)}, device_id_type=MESH
        )
    for k in range(1, n_xl):
        pl.semaphore_signal(
            barrier, inc=1, device_id={"xl": lax.rem(xl + k, n_xl)}, device_id_type=MESH
        )
    expected = n_inl - 1 + n_xl - 1
    for dr, dc in sides:
        if dr != 0 and dc != 0:
            there = exists(dr, dc)
            expected = expected + there.astype(jnp.int32)

            @pl.when(there)
            def _(dr=dr, dc=dc):
                pl.semaphore_signal(
                    barrier, inc=1, device_id={"inl": inl + dr, "xl": xl + dc}, device_id_type=MESH
                )

    s_hi[KROWS:KPAD, :] = jnp.zeros((KPAD - KROWS, 640), BF16)
    s_lo[KROWS:KPAD, :] = jnp.zeros((KPAD - KROWS, 640), BF16)
    pl.semaphore_wait(barrier, expected)

    def halo(n, dr, dc):
        return pltpu.make_async_remote_copy(
            src_ref=spectra_ref,
            dst_ref=block_ref.at[1 - dr, 1 - dc],
            send_sem=halo_send.at[n],
            recv_sem=halo_recv.at[n],
            device_id={"inl": inl + dr, "xl": xl + dc},
            device_id_type=MESH,
        )

    for n, (dr, dc) in enumerate(sides):

        @pl.when(exists(dr, dc))
        def _(n=n, dr=dr, dc=dc):
            halo(n, dr, dc).start()

    for dr, dc in sides:

        @pl.when(jnp.logical_not(exists(dr, dc)))
        def _(dr=dr, dc=dc):
            block_ref[1 + dr, 1 + dc] = jnp.zeros((2, 16, LANES), F32)

    block_ref[1, 1] = spectra_ref[...]

    prepare_weights(omega_ref, taps_ref, compact_ref, band_hi, band_lo)

    for n, (dr, dc) in enumerate(sides):

        @pl.when(exists(dr, dc))
        def _(n=n, dr=dr, dc=dc):
            halo(n, dr, dc).wait_send()

        @pl.when(exists(-dr, -dc))
        def _(n=n, dr=dr, dc=dc):
            halo(n, dr, dc).wait_recv()

    build_main(block_ref, s_hi, s_lo)

    def sketch_rows(shift, at, width):
        rows = slice(shift * CH, (shift + 1) * CH)
        left_hi = band_hi[rows, :]
        right = s_hi[:, at : at + width]
        return mm(left_hi, right) + mm(band_lo[rows, :], right) + mm(left_hi, s_lo[:, at : at + width])

    for shift in range(8):
        value = sketch_rows(shift, LANES, 2 * LANES)
        for half in range(2):
            sketch_ref[pl.ds(8 * half + shift, CH, stride=16), :] = value[
                :, half * LANES : (half + 1) * LANES
            ]
        high, low = split(value)
        y_hi[shift * CH : (shift + 1) * CH, 128:384] = high
        y_lo[shift * CH : (shift + 1) * CH, 128:384] = low

    copy_out = pltpu.make_async_copy(sketch_ref, sketch_out, out_sem)
    copy_out.start()

    main_hi, main_lo = s_hi[0:KROWS, 128:384], s_lo[0:KROWS, 128:384]
    prod_ref[KROWS : KROWS + 8, :] = jnp.zeros((8, 256), F32)
    total = None
    for pair in range(4):
        rows = slice(pair * 256, (pair + 1) * 256)
        own_hi = y_hi[rows, 128:384]
        prod_ref[0:KROWS, :] = (
            mm_t(main_hi, own_hi) + mm_t(main_lo, own_hi) + mm_t(main_hi, y_lo[rows, 128:384])
        )
        for k in range(2):
            term = prod_ref[2 * pair + k : 2 * pair + k + KROWS, k * LANES : (k + 1) * LANES]
            total = term if total is None else total + term
    prod_ref[0:KROWS, 0:LANES] = total
    first = prod_ref[0 : KROWS // 2, 0:LANES]
    second = prod_ref[KROWS // 2 : KROWS, 0:LANES]
    sign = jnp.where(lane_iota(1) < HALF, 1.0, -1.0)
    moments = roll(second, HALF) + first * sign
    for q in range(KI):
        send_ref[q * 16 : q * 16 + 16, :] = moments[q * WIN : q * WIN + 16]
        send_ref[272 + q : 273 + q, :] = moments[q * WIN + 16 : q * WIN + 17]
    send_ref[289:TROWS, :] = jnp.zeros((TROWS - 289, LANES), F32)

    def piece(at):
        return pl.ds(pl.multiple_of(at * share, 8), share)

    def scatter(k):
        peer = lax.rem(inl + k, n_inl)
        return pltpu.make_async_remote_copy(
            src_ref=send_ref.at[piece(peer)],
            dst_ref=recv_a.at[inl],
            send_sem=a_send.at[k],
            recv_sem=a_recv.at[k],
            device_id={"inl": peer},
            device_id_type=MESH,
        )

    def across(k):
        return pltpu.make_async_remote_copy(
            src_ref=part_ref,
            dst_ref=recv_b.at[xl],
            send_sem=b_send.at[k],
            recv_sem=b_recv.at[k],
            device_id={"xl": lax.rem(xl + k, n_xl)},
            device_id_type=MESH,
        )

    def gather(k):
        return pltpu.make_async_remote_copy(
            src_ref=full_ref,
            dst_ref=recv_c.at[inl],
            send_sem=c_send.at[k],
            recv_sem=c_recv.at[k],
            device_id={"inl": lax.rem(inl + k, n_inl)},
            device_id_type=MESH,
        )

    for k in range(1, n_inl):
        scatter(k).start()
    recv_a[inl] = send_ref[piece(inl), :]

    build_side(block_ref, s_hi, s_lo)
    side_lane = lane_iota(1)
    keep_up = up.astype(F32)
    keep_down = down.astype(F32)
    keep_side = jnp.where(side_lane % 16 < 8, west.astype(F32), east.astype(F32))
    keep = jnp.concatenate([jnp.full((1, LANES), keep_down), keep_side], axis=1)
    for shift in range(8):
        rows = slice(shift * CH, (shift + 1) * CH)
        high, low = split(sketch_rows(shift, 0, LANES) * keep_up)
        y_hi[rows, 0:128] = high
        y_lo[rows, 0:128] = low
        value = sketch_rows(shift, 384, 256)
        side = value[:, LANES:]
        side_keep = jnp.where(
            side_lane < 16, keep_up, jnp.where((side_lane >= 48) & (side_lane < 64), keep_down, 1.0)
        )
        high, low = split(value * keep * jnp.concatenate([jnp.ones((1, LANES), F32), side_keep], axis=1))
        y_hi[rows, 384:640] = high
        y_lo[rows, 384:640] = low

    for k in range(1, n_inl):
        scatter(k).wait()
    value = recv_a[0]
    for k in range(1, n_inl):
        value = value + recv_a[k]
    part_ref[...] = value
    for k in range(1, n_xl):
        across(k).start()
    recv_b[xl] = value
    for k in range(1, n_xl):
        across(k).wait()
    value = recv_b[0]
    for k in range(1, n_xl):
        value = value + recv_b[k]
    full_ref[...] = value
    for k in range(1, n_inl):
        gather(k).start()
    recv_c[inl] = value
    for k in range(1, n_inl):
        gather(k).wait()

    moments = recv_c[...].reshape(TROWS, LANES)
    products = mm_exact(moments.T, compact_ref[...])
    gram = products[:HALF] - roll(products[HALF:], HALF) * sign
    inverse = invert(gram)
    mixing = jnp.concatenate([inverse * sign, roll(inverse, HALF)], axis=0)
    coeffs = mm_exact(moments, mixing)

    spread_ref[:, 0:8, :] = jnp.zeros((GROUPS, 8, LANES), F32)
    spread_ref[:, 24:32, :] = jnp.zeros((GROUPS, 8, LANES), F32)
    for x, value in enumerate((coeffs * sign, roll(coeffs, HALF))):
        for q in range(KI):
            spread_ref[x * KI + q, 8:24, :] = value[q * 16 : q * 16 + 16]
            spread_ref[x * KI + q, 24:25, :] = value[272 + q : 273 + q]

    main = None
    edge = None
    for window in range(3):
        for shift in range(8):
            at = 8 + 8 * window - shift
            value = spread_ref[:, at : at + 8, :].reshape(GROUPS * 8, LANES)
            high, low = split(value)
            c_hi[:, shift * LANES : (shift + 1) * LANES] = high
            c_lo[:, shift * LANES : (shift + 1) * LANES] = low
        high, low = c_hi[...], c_lo[...]
        at = (2 - window) * LANES
        y = y_hi[:, at : at + 256]
        term = mm(high, y) + mm(low, y) + mm(high, y_lo[:, at : at + 256])
        main = term if main is None else main + term
        y = y_hi[:, 512:640]
        term = mm(high, y) + mm(low, y) + mm(high, y_lo[:, 512:640])
        term = roll(term, 16 * (window - 2))
        edge = term if edge is None else edge + term

    lane = lane_iota(8)
    sub = lax.broadcasted_iota(jnp.int32, (8, LANES), 0)
    count_j = counts(xl * LANES, LANES, n_xl * LANES, lane)
    for x in range(2):
        for h in range(2):
            total = None
            for q in range(KI):
                s = q - HW
                rows = slice((x * KI + q) * 8, (x * KI + q) * 8 + 8)
                value = roll(main[rows, h * LANES : (h + 1) * LANES], s)
                if s != 0:
                    outer = roll(edge[rows, :], s - 8 - 16 * h)
                    value = jnp.where(lane < s if s > 0 else lane >= LANES + s, outer, value)
                total = value if total is None else total + value
            count_i = counts(inl * 16 + 8 * h, 16, n_inl * 16, sub)
            denoised_ref[x, 8 * h : 8 * h + 8, :] = total / (count_i * count_j)

    copy_out.wait()


def per_device(n_inl, n_xl, spectra, omega):
    share = TROWS // n_inl
    vmem = pltpu.VMEM
    dma = pltpu.SemaphoreType.DMA
    sketch, denoised = pl.pallas_call(
        functools.partial(kernel, n_inl, n_xl),
        out_shape=(
            jax.ShapeDtypeStruct((CH * 16, LANES), F32),
            jax.ShapeDtypeStruct((2, 16, LANES), F32),
        ),
        in_specs=[pl.BlockSpec(memory_space=pltpu.VMEM)] * 2,
        out_specs=(pl.BlockSpec(memory_space=pl.ANY), pl.BlockSpec(memory_space=pltpu.VMEM)),
        scratch_shapes=[
            vmem((3, 3, 2, 16, LANES), F32),
            vmem((TROWS, LANES), F32),
            vmem((TROWS, LANES), F32),
            vmem((8 * CH, KPAD), BF16),
            vmem((8 * CH, KPAD), BF16),
            vmem((KPAD, 640), BF16),
            vmem((KPAD, 640), BF16),
            vmem((8 * CH, 640), BF16),
            vmem((8 * CH, 640), BF16),
            vmem((CH * 16, LANES), F32),
            vmem((KROWS + 8, 256), F32),
            vmem((TROWS, LANES), F32),
            vmem((n_inl, share, LANES), F32),
            vmem((share, LANES), F32),
            vmem((n_xl, share, LANES), F32),
            vmem((share, LANES), F32),
            vmem((n_inl, share, LANES), F32),
            vmem((GROUPS, 32, LANES), F32),
            vmem((GROUPS * 8, 8 * LANES), BF16),
            vmem((GROUPS * 8, 8 * LANES), BF16),
            dma((8,)),
            dma((8,)),
            dma((n_inl,)),
            dma((n_inl,)),
            dma((n_xl,)),
            dma((n_xl,)),
            dma((n_inl,)),
            dma((n_inl,)),
            dma,
        ],
        compiler_params=pltpu.CompilerParams(
            collective_id=0, has_side_effects=True, vmem_limit_bytes=48 * 1024 * 1024
        ),
    )(spectra[0], omega)
    return sketch.reshape(1, CH, 16, LANES), denoised[None]


def solution(mesh):
    in_specs = (P("freq", None, "inl", "xl"), P())
    out_specs = (P("freq", None, "inl", "xl"), P("freq", None, "inl", "xl"))
    return jax.shard_map(
        functools.partial(per_device, mesh.shape["inl"], mesh.shape["xl"]),
        mesh=mesh,
        in_specs=in_specs,
        out_specs=out_specs,
        check_vma=False,
    )
```

```python
import functools

import jax
import jax.numpy as jnp
from jax import lax
from jax.experimental import pallas as pl
from jax.experimental.pallas import tpu as pltpu
from jax.sharding import PartitionSpec as P

MESH = pl.DeviceIdType.MESH
F32 = jnp.float32
BF16 = jnp.bfloat16
KI = 17
HW = 8
WIN = 24
GROUPS = 2 * KI
KROWS = GROUPS * WIN
KPAD = 896
TROWS = 384
LANES = 128
CH = 128
HALF = 64


def split(value):
    high = value.astype(BF16)
    return high, (value - high.astype(F32)).astype(BF16)


def mm(a, b):
    return jnp.dot(a, b, preferred_element_type=F32)


def mm_exact(a, b):
    return jnp.dot(a, b, preferred_element_type=F32, precision=lax.Precision.HIGHEST)


def mm_t(a, b):
    return lax.dot_general(a, b, (((1,), (1,)), ((), ())), preferred_element_type=F32)


def roll(value, amount, axis=1):
    size = value.shape[axis]
    amount = amount % size
    return value if amount == 0 else pltpu.roll(value, amount, axis)


def lane_iota(rows, lanes=LANES):
    return lax.broadcasted_iota(jnp.int32, (rows, lanes), 1)


def prepare_weights(omega_ref, taps_ref, band_hi, band_lo):
    taps_ref[:, 256:TROWS] = jnp.zeros((CH, TROWS - 256), F32)
    taps_ref[0:HALF, 0 : KI * KI] = omega_ref[0]
    taps_ref[HALF:CH, 0 : KI * KI] = omega_ref[1]
    tap_t = taps_ref[...]
    turned = jnp.concatenate([-tap_t[HALF:], tap_t[:HALF]], axis=0)
    col = lane_iota(1, KPAD)
    second = col >= KROWS // 2
    inner = jnp.where(second, col - KROWS // 2, col)
    q = (inner * 2731) >> 16
    r = inner - q * WIN
    tap = jnp.where((r < KI) & (col < KROWS), r * KI + q, -1)
    row = lax.broadcasted_iota(jnp.int32, (TROWS, KPAD), 0)
    pick_re = (row == jnp.where(second, -1, tap)).astype(F32).astype(BF16)
    pick_im = (row == jnp.where(second, tap, -1)).astype(F32).astype(BF16)
    re_hi, re_lo = split(tap_t)
    im_hi, im_lo = split(turned)
    wide_hi = mm(re_hi, pick_re) + mm(im_hi, pick_im)
    wide_lo = mm(re_lo, pick_re) + mm(im_lo, pick_im)
    for shift in range(8):
        band_hi[shift * CH : (shift + 1) * CH, :] = roll(wide_hi, shift).astype(BF16)
        band_lo[shift * CH : (shift + 1) * CH, :] = roll(wide_lo, shift).astype(BF16)


def shifted(left, centre, right, s, lane):
    if s == 0:
        return centre
    if s < 0:
        return jnp.where(lane < -s, roll(left, -s), roll(centre, -s))
    return jnp.where(lane >= LANES - s, roll(right, LANES - s), roll(centre, LANES - s))


def plane(block_ref, x, dc):
    return jnp.concatenate([block_ref[dr, dc, x] for dr in range(3)], axis=0)


def build_main(block_ref, s_hi, s_lo):
    lane = lane_iota(48)
    windows = []
    for x in range(2):
        left, centre, right = (plane(block_ref, x, dc) for dc in range(3))
        for q in range(KI):
            windows.append(shifted(left, centre, right, q - HW, lane))
    for k in range(KI):
        first, second = windows[2 * k], windows[2 * k + 1]
        for g in range(4):
            value = jnp.concatenate([first[8 * g : 8 * g + WIN], second[8 * g : 8 * g + WIN]], axis=0)
            high, low = split(value)
            s_hi[48 * k : 48 * k + 48, g * LANES : (g + 1) * LANES] = high
            s_lo[48 * k : 48 * k + 48, g * LANES : (g + 1) * LANES] = low


def build_side(block_ref, s_hi, s_lo):
    lane = lane_iota(48)
    strips = []
    for x in range(2):
        left, centre, right = (plane(block_ref, x, dc) for dc in range(3))
        for q in range(KI):
            inner = roll(centre, 16 - q)
            near = lane < 16 - q
            strip = jnp.where(
                lane < 8,
                jnp.where(near, roll(left, 16 - q), inner),
                jnp.where(near, inner, roll(right, 16 - q)),
            )
            strip = jnp.where(lane < 16, strip, 0.0)
            total = strip[0:WIN]
            for g in range(1, 4):
                total = total + roll(strip[8 * g : 8 * g + WIN], 16 * g)
            strips.append(total)
    for k in range(KI):
        high, low = split(jnp.concatenate([strips[2 * k], strips[2 * k + 1]], axis=0))
        s_hi[48 * k : 48 * k + 48, 512:640] = high
        s_lo[48 * k : 48 * k + 48, 512:640] = low


def invert(matrix):
    shape = (8, LANES)
    lane = lane_iota(8)
    pair = (lane & (HALF - 1)) >> 1
    sub = lax.broadcasted_iota(jnp.int32, shape, 0)
    turn = jnp.where(lane < HALF, -1.0, 1.0)
    tiles = [matrix[8 * v : 8 * v + 8] for v in range(HALF // 8)]

    def fill(value):
        return jnp.broadcast_to(value, shape)

    for k in range(0, HALF, 2):
        v, r = divmod(k, 8)
        row1, row2 = fill(tiles[v][r : r + 1, :]), fill(tiles[v][r + 1 : r + 2, :])
        a, d = fill(row1[:, k : k + 1]), fill(row2[:, k + 1 : k + 2])
        br, bi = fill(row1[:, k + 1 : k + 2]), fill(row1[:, HALF + k + 1 : HALF + k + 2])
        cut = pair == k // 2
        row1 = jnp.where(cut, jnp.where(lane == k, 1.0, 0.0), row1)
        row2 = jnp.where(cut, jnp.where(lane == k + 1, 1.0, 0.0), row2)
        turned1, turned2 = roll(row1, HALF) * turn, roll(row2, HALF) * turn
        p1 = 1.0 / a
        er, ei = br * p1, bi * p1
        p2 = 1.0 / (d - (br * er + bi * ei))
        new2 = p2 * (row2 - (er * row1 - ei * turned1))
        spun2 = p2 * (turned2 - (er * turned1 + ei * row1))
        new1 = p1 * row1 - (er * new2 + ei * spun2)
        spun1 = p1 * turned1 - (er * spun2 - ei * new2)
        after = []
        for w, tile in enumerate(tiles):
            first = fill(tile[:, k : k + 1]) * new1 + fill(tile[:, HALF + k : HALF + k + 1]) * spun1
            second = (
                fill(tile[:, k + 1 : k + 2]) * new2
                + fill(tile[:, HALF + k + 1 : HALF + k + 2]) * spun2
            )
            value = jnp.where(cut, 0.0, tile) - (first + second)
            if w == v:
                value = jnp.where(sub == r, new1, jnp.where(sub == r + 1, new2, value))
            after.append(value)
        tiles = after
    return jnp.concatenate(tiles, axis=0)


def counts(start, length, total, index):
    at = start + index
    return (jnp.minimum(at + HW, total - 1) - jnp.maximum(at - HW, 0) + 1).astype(F32)


def gather_kernel(
    n_inl,
    n_xl,
    spectra_ref,
    omega_hbm,
    sketch_ref,
    moments_ref,
    inverse_ref,
    y_hi,
    y_lo,
    block_ref,
    omega_ref,
    taps_ref,
    band_hi,
    band_lo,
    s_hi,
    s_lo,
    prod_ref,
    send_ref,
    gram_ref,
    gram_b,
    gram_part,
    gram_c,
    recv_a,
    part_ref,
    recv_b,
    full_ref,
    recv_c,
    halo_send,
    halo_recv,
    a_send,
    a_recv,
    b_send,
    b_recv,
    c_send,
    c_recv,
    gb_send,
    gb_recv,
    gc_send,
    gc_recv,
    own_sem,
    omega_sem,
):
    own_copy = pltpu.make_async_copy(spectra_ref, block_ref.at[1, 1], own_sem)
    own_copy.start()
    omega_copy = pltpu.make_async_copy(omega_hbm, omega_ref, omega_sem)
    omega_copy.start()
    inl = lax.axis_index("inl")
    xl = lax.axis_index("xl")
    up, down = inl > 0, inl < n_inl - 1
    west, east = xl > 0, xl < n_xl - 1
    barrier = pltpu.get_barrier_semaphore()
    sides = [(dr, dc) for dr in (-1, 0, 1) for dc in (-1, 0, 1) if (dr, dc) != (0, 0)]

    def exists(dr, dc):
        ok = None
        for step, low, high in ((dr, up, down), (dc, west, east)):
            if step != 0:
                one = low if step < 0 else high
                ok = one if ok is None else ok & one
        return ok

    for k in range(1, n_inl):
        pl.semaphore_signal(
            barrier, inc=1, device_id={"inl": lax.rem(inl + k, n_inl)}, device_id_type=MESH
        )
    for k in range(1, n_xl):
        pl.semaphore_signal(
            barrier, inc=1, device_id={"xl": lax.rem(xl + k, n_xl)}, device_id_type=MESH
        )
    expected = n_inl - 1 + n_xl - 1
    for dr, dc in sides:
        if dr != 0 and dc != 0:
            there = exists(dr, dc)
            expected = expected + there.astype(jnp.int32)

            @pl.when(there)
            def _(dr=dr, dc=dc):
                pl.semaphore_signal(
                    barrier, inc=1, device_id={"inl": inl + dr, "xl": xl + dc}, device_id_type=MESH
                )

    s_hi[KROWS:KPAD, :] = jnp.zeros((KPAD - KROWS, 640), BF16)
    s_lo[KROWS:KPAD, :] = jnp.zeros((KPAD - KROWS, 640), BF16)
    pl.semaphore_wait(barrier, expected)

    def halo(n, dr, dc):
        return pltpu.make_async_remote_copy(
            src_ref=spectra_ref,
            dst_ref=block_ref.at[1 - dr, 1 - dc],
            send_sem=halo_send.at[n],
            recv_sem=halo_recv.at[n],
            device_id={"inl": inl + dr, "xl": xl + dc},
            device_id_type=MESH,
        )

    for n, (dr, dc) in enumerate(sides):

        @pl.when(exists(dr, dc))
        def _(n=n, dr=dr, dc=dc):
            halo(n, dr, dc).start()

    for dr, dc in sides:

        @pl.when(jnp.logical_not(exists(dr, dc)))
        def _(dr=dr, dc=dc):
            block_ref[1 + dr, 1 + dc] = jnp.zeros((2, 16, LANES), F32)

    omega_copy.wait()
    prepare_weights(omega_ref, taps_ref, band_hi, band_lo)

    own_copy.wait()
    for n, (dr, dc) in enumerate(sides):

        @pl.when(exists(dr, dc))
        def _(n=n, dr=dr, dc=dc):
            halo(n, dr, dc).wait_send()

        @pl.when(exists(-dr, -dc))
        def _(n=n, dr=dr, dc=dc):
            halo(n, dr, dc).wait_recv()

    build_main(block_ref, s_hi, s_lo)

    def sketch_rows(shift, at, width):
        rows = slice(shift * CH, (shift + 1) * CH)
        left_hi = band_hi[rows, :]
        right = s_hi[:, at : at + width]
        return mm(left_hi, right) + mm(band_lo[rows, :], right) + mm(left_hi, s_lo[:, at : at + width])

    for shift in range(8):
        value = sketch_rows(shift, LANES, 2 * LANES)
        for half in range(2):
            sketch_ref[pl.ds(8 * half + shift, CH, stride=16), :] = value[
                :, half * LANES : (half + 1) * LANES
            ]
        high, low = split(value)
        y_hi[shift * CH : (shift + 1) * CH, 128:384] = high
        y_lo[shift * CH : (shift + 1) * CH, 128:384] = low

    sums = None
    for shift in range(8):
        rows = slice(shift * CH, (shift + 1) * CH)
        high = y_hi[rows, 128:384]
        term = mm_t(jnp.concatenate([high, y_lo[rows, 128:384]], axis=0), high)
        sums = term if sums is None else sums + term
    sign = jnp.where(lane_iota(1) < HALF, 1.0, -1.0)
    products = sums[:CH] + (sums[CH:] + sums[CH:].T)
    gram = products[:HALF] + roll(products[HALF:], HALF) * sign
    lane = lane_iota(HALF)
    sub = lax.broadcasted_iota(jnp.int32, (HALF, LANES), 0)
    gram = jnp.where(sub >= lane, gram, roll(gram, HALF))
    gram_ref[...] = jnp.where(lane[:32] < HALF, gram[:32], roll(gram[32:], HALF))

    def piece(at):
        share = TROWS // n_inl
        return pl.ds(pl.multiple_of(at * share, 8), share)

    def exchange(axis, source, slots, sems):
        me, count = (inl, n_inl) if axis == "inl" else (xl, n_xl)
        send, recv = sems
        pieces = source.shape[0] != slots.shape[1]

        def copy(k):
            peer = lax.rem(me + k, count)
            return pltpu.make_async_remote_copy(
                src_ref=source.at[piece(peer)] if pieces else source,
                dst_ref=slots.at[me],
                send_sem=send.at[k],
                recv_sem=recv.at[k],
                device_id={axis: peer},
                device_id_type=MESH,
            )

        def start():
            for k in range(1, count):
                copy(k).start()
            slots[me] = source[piece(me), :] if pieces else source[...]

        def wait():
            for k in range(1, count):
                copy(k).wait()

        return start, wait

    def summed(slots):
        values = [slots[k] for k in range(slots.shape[0])]
        while len(values) > 1:
            values = [a + b for a, b in zip(values[::2], values[1::2])]
        return values[0]

    gram_xl = exchange("xl", gram_ref, gram_b, (gb_send, gb_recv))
    gram_inl = exchange("inl", gram_part, gram_c, (gc_send, gc_recv))
    scatter_inl = exchange("inl", send_ref, recv_a, (a_send, a_recv))
    across_xl = exchange("xl", part_ref, recv_b, (b_send, b_recv))
    gather_inl = exchange("inl", full_ref, recv_c, (c_send, c_recv))
    gram_xl[0]()

    main_hi, main_lo = s_hi[0:KROWS, 128:384], s_lo[0:KROWS, 128:384]
    prod_ref[KROWS : KROWS + 8, :] = jnp.zeros((8, 256), F32)
    total = None
    for pair in range(4):
        rows = slice(pair * 256, (pair + 1) * 256)
        own_hi = y_hi[rows, 128:384]
        prod_ref[0:KROWS, :] = (
            mm_t(main_hi, own_hi) + mm_t(main_lo, own_hi) + mm_t(main_hi, y_lo[rows, 128:384])
        )
        for k in range(2):
            term = prod_ref[2 * pair + k : 2 * pair + k + KROWS, k * LANES : (k + 1) * LANES]
            total = term if total is None else total + term
    prod_ref[0:KROWS, 0:LANES] = total
    first = prod_ref[0 : KROWS // 2, 0:LANES]
    second = prod_ref[KROWS // 2 : KROWS, 0:LANES]
    moments = roll(second, HALF) + first * sign
    for q in range(KI):
        send_ref[q * 16 : q * 16 + 16, :] = moments[q * WIN : q * WIN + 16]
        send_ref[272 + q : 273 + q, :] = moments[q * WIN + 16 : q * WIN + 17]
    send_ref[289:TROWS, :] = jnp.zeros((TROWS - 289, LANES), F32)

    scatter_inl[0]()

    build_side(block_ref, s_hi, s_lo)

    side_lane = lane_iota(1)
    keep_up = up.astype(F32)
    keep_down = down.astype(F32)
    keep_side = jnp.where(side_lane % 16 < 8, west.astype(F32), east.astype(F32)) * jnp.where(
        side_lane < 16, keep_up, jnp.where((side_lane >= 48) & (side_lane < 64), keep_down, 1.0)
    )
    keep = jnp.concatenate([jnp.full((1, LANES), keep_down), keep_side], axis=1)

    def outer_rows(shift):
        rows = slice(shift * CH, (shift + 1) * CH)
        high, low = split(sketch_rows(shift, 0, LANES) * keep_up)
        y_hi[rows, 0:128] = high
        y_lo[rows, 0:128] = low
        high, low = split(sketch_rows(shift, 384, 256) * keep)
        y_hi[rows, 384:640] = high
        y_lo[rows, 384:640] = low

    for shift in range(4):
        outer_rows(shift)
    gram_xl[1]()
    gram_part[...] = summed(gram_b)
    gram_inl[0]()
    for shift in range(4, 8):
        outer_rows(shift)
    scatter_inl[1]()
    part_ref[...] = summed(recv_a)
    across_xl[0]()
    gram_inl[1]()
    packed = summed(gram_c)
    packed = jnp.concatenate([packed, roll(packed, HALF)], axis=0)
    flipped = jnp.concatenate([packed, jnp.zeros_like(packed)], axis=0).T[:HALF]
    real = jnp.where(sub >= lane, packed, flipped)
    imag = jnp.where(sub < lane, packed, jnp.where(sub > lane, -flipped, 0.0))
    gram = jnp.where(lane < HALF, real, roll(imag, HALF))
    across_xl[1]()
    full_ref[...] = summed(recv_b)
    gather_inl[0]()
    inverse_ref[...] = invert(gram)
    gather_inl[1]()
    moments_ref[...] = recv_c[...].reshape(TROWS, LANES)


def spread_kernel(
    n_inl,
    n_xl,
    sketch_ref,
    moments_ref,
    inverse_ref,
    y_hi,
    y_lo,
    sketch_out,
    denoised_ref,
    spread_ref,
    c_hi,
    c_lo,
    out_sem,
):
    inl = lax.axis_index("inl")
    xl = lax.axis_index("xl")
    copy_out = pltpu.make_async_copy(sketch_ref, sketch_out, out_sem)
    copy_out.start()
    sign = jnp.where(lane_iota(1) < HALF, 1.0, -1.0)
    inverse = inverse_ref[...]
    mixing = jnp.concatenate([inverse * sign, roll(inverse, HALF)], axis=0)
    coeffs = mm_exact(moments_ref[...], mixing)

    spread_ref[:, 0:8, :] = jnp.zeros((GROUPS, 8, LANES), F32)
    spread_ref[:, 24:32, :] = jnp.zeros((GROUPS, 8, LANES), F32)
    for x, value in enumerate((coeffs * sign, roll(coeffs, HALF))):
        for q in range(KI):
            spread_ref[x * KI + q, 8:24, :] = value[q * 16 : q * 16 + 16]
            spread_ref[x * KI + q, 24:25, :] = value[272 + q : 273 + q]

    main = None
    edge = None
    for window in range(3):
        for shift in range(8):
            at = 8 + 8 * window - shift
            value = spread_ref[:, at : at + 8, :].reshape(GROUPS * 8, LANES)
            high, low = split(value)
            c_hi[:, shift * LANES : (shift + 1) * LANES] = high
            c_lo[:, shift * LANES : (shift + 1) * LANES] = low
        high, low = c_hi[...], c_lo[...]
        at = (2 - window) * LANES
        y = y_hi[:, at : at + 256]
        term = mm(high, y) + mm(low, y) + mm(high, y_lo[:, at : at + 256])
        main = term if main is None else main + term
        y = y_hi[:, 512:640]
        term = mm(high, y) + mm(low, y) + mm(high, y_lo[:, 512:640])
        term = roll(term, 16 * (window - 2))
        edge = term if edge is None else edge + term

    copy_out.wait()
    lane = lane_iota(8)
    sub = lax.broadcasted_iota(jnp.int32, (8, LANES), 0)
    count_j = counts(xl * LANES, LANES, n_xl * LANES, lane)
    for x in range(2):
        for h in range(2):
            total = None
            for q in range(KI):
                s = q - HW
                rows = slice((x * KI + q) * 8, (x * KI + q) * 8 + 8)
                value = roll(main[rows, h * LANES : (h + 1) * LANES], s)
                if s != 0:
                    outer = roll(edge[rows, :], s - 8 - 16 * h)
                    value = jnp.where(lane < s if s > 0 else lane >= LANES + s, outer, value)
                total = value if total is None else total + value
            count_i = counts(inl * 16 + 8 * h, 16, n_inl * 16, sub)
            denoised_ref[x, 8 * h : 8 * h + 8, :] = total / (count_i * count_j)


def per_device(n_inl, n_xl, spectra, omega):
    vmem = pltpu.VMEM
    dma = pltpu.SemaphoreType.DMA
    here = pl.BlockSpec(memory_space=pltpu.VMEM)
    anywhere = pl.BlockSpec(memory_space=pl.ANY)
    limit = 24 * 1024 * 1024

    share = TROWS // n_inl
    inl_sems = [dma((n_inl,))] * 2
    xl_sems = [dma((n_xl,))] * 2
    results = pl.pallas_call(
        functools.partial(gather_kernel, n_inl, n_xl),
        out_shape=(
            jax.ShapeDtypeStruct((CH * 16, LANES), F32),
            jax.ShapeDtypeStruct((TROWS, LANES), F32),
            jax.ShapeDtypeStruct((HALF, LANES), F32),
            jax.ShapeDtypeStruct((8 * CH, 640), BF16),
            jax.ShapeDtypeStruct((8 * CH, 640), BF16),
        ),
        in_specs=[pl.BlockSpec(memory_space=pltpu.HBM)] * 2,
        out_specs=(here,) * 5,
        scratch_shapes=[
            vmem((3, 3, 2, 16, LANES), F32),
            vmem((2, HALF, KI * KI), F32),
            vmem((CH, TROWS), F32),
            vmem((8 * CH, KPAD), BF16),
            vmem((8 * CH, KPAD), BF16),
            vmem((KPAD, 640), BF16),
            vmem((KPAD, 640), BF16),
            vmem((KROWS + 8, 256), F32),
            vmem((TROWS, LANES), F32),
            vmem((32, LANES), F32),
            vmem((n_xl, 32, LANES), F32),
            vmem((32, LANES), F32),
            vmem((n_inl, 32, LANES), F32),
            vmem((n_inl, share, LANES), F32),
            vmem((share, LANES), F32),
            vmem((n_xl, share, LANES), F32),
            vmem((share, LANES), F32),
            vmem((n_inl, share, LANES), F32),
            dma((8,)),
            dma((8,)),
            *inl_sems,
            *xl_sems,
            *inl_sems,
            *xl_sems,
            *inl_sems,
            dma,
            dma,
        ],
        compiler_params=pltpu.CompilerParams(
            collective_id=0, has_side_effects=True, vmem_limit_bytes=limit
        ),
    )(
        pltpu.with_memory_space_constraint(spectra[0], pltpu.HBM),
        pltpu.with_memory_space_constraint(omega.transpose(0, 2, 1), pltpu.HBM),
    )
    sketch, denoised = pl.pallas_call(
        functools.partial(spread_kernel, n_inl, n_xl),
        out_shape=(
            jax.ShapeDtypeStruct((CH * 16, LANES), F32),
            jax.ShapeDtypeStruct((2, 16, LANES), F32),
        ),
        in_specs=[anywhere] + [here] * 4,
        out_specs=(anywhere, here),
        scratch_shapes=[
            vmem((GROUPS, 32, LANES), F32),
            vmem((GROUPS * 8, 8 * LANES), BF16),
            vmem((GROUPS * 8, 8 * LANES), BF16),
            dma,
        ],
        compiler_params=pltpu.CompilerParams(vmem_limit_bytes=limit),
    )(*results)
    return sketch.reshape(1, CH, 16, LANES), denoised[None]


def solution(mesh):
    in_specs = (P("freq", None, "inl", "xl"), P())
    out_specs = (P("freq", None, "inl", "xl"), P("freq", None, "inl", "xl"))
    return jax.shard_map(
        functools.partial(per_device, mesh.shape["inl"], mesh.shape["xl"]),
        mesh=mesh,
        in_specs=in_specs,
        out_specs=out_specs,
        check_vma=False,
    )
```

```python
import functools

import jax
import jax.numpy as jnp
from jax import lax
from jax.experimental import pallas as pl
from jax.experimental.pallas import tpu as pltpu
from jax.sharding import PartitionSpec as P

MESH = pl.DeviceIdType.MESH
F32 = jnp.float32
BF16 = jnp.bfloat16
KI = 17
HW = 8
WIN = 24
GROUPS = 2 * KI
KROWS = GROUPS * WIN
KPAD = 896
TROWS = 384
LANES = 128
CH = 128
HALF = 64


def split(value):
    high = value.astype(BF16)
    return high, (value - high.astype(F32)).astype(BF16)


def mm(a, b):
    return jnp.dot(a, b, preferred_element_type=F32)


def mm_exact(a, b):
    return jnp.dot(a, b, preferred_element_type=F32, precision=lax.Precision.HIGHEST)


def mm_t(a, b):
    return lax.dot_general(a, b, (((1,), (1,)), ((), ())), preferred_element_type=F32)


def roll(value, amount, axis=1):
    size = value.shape[axis]
    amount = amount % size
    return value if amount == 0 else pltpu.roll(value, amount, axis)


def lane_iota(rows, lanes=LANES):
    return lax.broadcasted_iota(jnp.int32, (rows, lanes), 1)


def prepare_weights(omega_ref, taps_ref, band_hi, band_lo):
    taps_ref[:, 256:TROWS] = jnp.zeros((CH, TROWS - 256), F32)
    taps_ref[0:HALF, 0 : KI * KI] = omega_ref[0]
    taps_ref[HALF:CH, 0 : KI * KI] = omega_ref[1]
    tap_t = taps_ref[...]
    turned = jnp.concatenate([-tap_t[HALF:], tap_t[:HALF]], axis=0)
    col = lane_iota(1, KPAD)
    second = col >= KROWS // 2
    inner = jnp.where(second, col - KROWS // 2, col)
    q = (inner * 2731) >> 16
    r = inner - q * WIN
    tap = jnp.where((r < KI) & (col < KROWS), r * KI + q, -1)
    row = lax.broadcasted_iota(jnp.int32, (TROWS, KPAD), 0)
    pick_re = (row == jnp.where(second, -1, tap)).astype(F32).astype(BF16)
    pick_im = (row == jnp.where(second, tap, -1)).astype(F32).astype(BF16)
    re_hi, re_lo = split(tap_t)
    im_hi, im_lo = split(turned)
    wide_hi = mm(re_hi, pick_re) + mm(im_hi, pick_im)
    wide_lo = mm(re_lo, pick_re) + mm(im_lo, pick_im)
    for shift in range(8):
        band_hi[shift * CH : (shift + 1) * CH, :] = roll(wide_hi, shift).astype(BF16)
        band_lo[shift * CH : (shift + 1) * CH, :] = roll(wide_lo, shift).astype(BF16)


def shifted(left, centre, right, s, lane):
    if s == 0:
        return centre
    if s < 0:
        return jnp.where(lane < -s, roll(left, -s), roll(centre, -s))
    return jnp.where(lane >= LANES - s, roll(right, LANES - s), roll(centre, LANES - s))


def plane(block_ref, x, dc):
    return jnp.concatenate([block_ref[dr, dc, x] for dr in range(3)], axis=0)


def build_main(block_ref, s_hi, s_lo):
    lane = lane_iota(48)
    windows = []
    for x in range(2):
        left, centre, right = (plane(block_ref, x, dc) for dc in range(3))
        for q in range(KI):
            windows.append(shifted(left, centre, right, q - HW, lane))
    for k in range(KI):
        first, second = windows[2 * k], windows[2 * k + 1]
        for g in range(4):
            value = jnp.concatenate([first[8 * g : 8 * g + WIN], second[8 * g : 8 * g + WIN]], axis=0)
            high, low = split(value)
            s_hi[48 * k : 48 * k + 48, g * LANES : (g + 1) * LANES] = high
            s_lo[48 * k : 48 * k + 48, g * LANES : (g + 1) * LANES] = low


def build_side(block_ref, s_hi, s_lo):
    lane = lane_iota(48)
    strips = []
    for x in range(2):
        left, centre, right = (plane(block_ref, x, dc) for dc in range(3))
        for q in range(KI):
            inner = roll(centre, 16 - q)
            near = lane < 16 - q
            strip = jnp.where(
                lane < 8,
                jnp.where(near, roll(left, 16 - q), inner),
                jnp.where(near, inner, roll(right, 16 - q)),
            )
            strip = jnp.where(lane < 16, strip, 0.0)
            total = strip[0:WIN]
            for g in range(1, 4):
                total = total + roll(strip[8 * g : 8 * g + WIN], 16 * g)
            strips.append(total)
    for k in range(KI):
        high, low = split(jnp.concatenate([strips[2 * k], strips[2 * k + 1]], axis=0))
        s_hi[48 * k : 48 * k + 48, 512:640] = high
        s_lo[48 * k : 48 * k + 48, 512:640] = low


def invert(matrix):
    shape = (8, LANES)
    lane = lane_iota(8)
    pair = (lane & (HALF - 1)) >> 1
    sub = lax.broadcasted_iota(jnp.int32, shape, 0)
    turn = jnp.where(lane < HALF, -1.0, 1.0)
    tiles = [matrix[8 * v : 8 * v + 8] for v in range(HALF // 8)]

    def fill(value):
        return jnp.broadcast_to(value, shape)

    for k in range(0, HALF, 2):
        v, r = divmod(k, 8)
        row1, row2 = fill(tiles[v][r : r + 1, :]), fill(tiles[v][r + 1 : r + 2, :])
        a, d = fill(row1[:, k : k + 1]), fill(row2[:, k + 1 : k + 2])
        br, bi = fill(row1[:, k + 1 : k + 2]), fill(row1[:, HALF + k + 1 : HALF + k + 2])
        cut = pair == k // 2
        row1 = jnp.where(cut, jnp.where(lane == k, 1.0, 0.0), row1)
        row2 = jnp.where(cut, jnp.where(lane == k + 1, 1.0, 0.0), row2)
        turned1, turned2 = roll(row1, HALF) * turn, roll(row2, HALF) * turn
        p1 = 1.0 / a
        er, ei = br * p1, bi * p1
        p2 = 1.0 / (d - (br * er + bi * ei))
        new2 = p2 * (row2 - (er * row1 - ei * turned1))
        spun2 = p2 * (turned2 - (er * turned1 + ei * row1))
        new1 = p1 * row1 - (er * new2 + ei * spun2)
        spun1 = p1 * turned1 - (er * spun2 - ei * new2)
        after = []
        for w, tile in enumerate(tiles):
            first = fill(tile[:, k : k + 1]) * new1 + fill(tile[:, HALF + k : HALF + k + 1]) * spun1
            second = (
                fill(tile[:, k + 1 : k + 2]) * new2
                + fill(tile[:, HALF + k + 1 : HALF + k + 2]) * spun2
            )
            value = jnp.where(cut, 0.0, tile) - (first + second)
            if w == v:
                value = jnp.where(sub == r, new1, jnp.where(sub == r + 1, new2, value))
            after.append(value)
        tiles = after
    return jnp.concatenate(tiles, axis=0)


def counts(start, length, total, index):
    at = start + index
    return (jnp.minimum(at + HW, total - 1) - jnp.maximum(at - HW, 0) + 1).astype(F32)


def gather_kernel(
    n_inl,
    n_xl,
    spectra_ref,
    omega_hbm,
    sketch_ref,
    moments_ref,
    inverse_ref,
    y_hi,
    y_lo,
    block_ref,
    omega_ref,
    taps_ref,
    band_hi,
    band_lo,
    s_hi,
    s_lo,
    prod_ref,
    send_ref,
    gram_ref,
    gram_b,
    gram_part,
    gram_c,
    matrix_ref,
    recv_a,
    part_ref,
    recv_b,
    full_ref,
    recv_c,
    halo_send,
    halo_recv,
    a_send,
    a_recv,
    b_send,
    b_recv,
    c_send,
    c_recv,
    gb_send,
    gb_recv,
    gc_send,
    gc_recv,
    own_sem,
    omega_sem,
):
    own_copy = pltpu.make_async_copy(spectra_ref, block_ref.at[1, 1], own_sem)
    own_copy.start()
    omega_copy = pltpu.make_async_copy(omega_hbm, omega_ref, omega_sem)
    omega_copy.start()
    inl = lax.axis_index("inl")
    xl = lax.axis_index("xl")
    up, down = inl > 0, inl < n_inl - 1
    west, east = xl > 0, xl < n_xl - 1
    barrier = pltpu.get_barrier_semaphore()
    sides = [(dr, dc) for dr in (-1, 0, 1) for dc in (-1, 0, 1) if (dr, dc) != (0, 0)]

    def exists(dr, dc):
        ok = None
        for step, low, high in ((dr, up, down), (dc, west, east)):
            if step != 0:
                one = low if step < 0 else high
                ok = one if ok is None else ok & one
        return ok

    def greet(axis, steps):
        me, count = (inl, n_inl) if axis == "inl" else (xl, n_xl)
        for k in steps:
            pl.semaphore_signal(
                barrier, inc=1, device_id={axis: lax.rem(me + k, count)}, device_id_type=MESH
            )

    greet("inl", sorted({1, n_inl - 1}))
    greet("xl", sorted({1, n_xl - 1}))
    expected = n_inl - 1 + n_xl - 1
    for dr, dc in sides:
        if dr != 0 and dc != 0:
            there = exists(dr, dc)
            expected = expected + there.astype(jnp.int32)

            @pl.when(there)
            def _(dr=dr, dc=dc):
                pl.semaphore_signal(
                    barrier, inc=1, device_id={"inl": inl + dr, "xl": xl + dc}, device_id_type=MESH
                )

    greet("inl", range(2, n_inl - 1))
    greet("xl", range(2, n_xl - 1))
    s_hi[KROWS:KPAD, :] = jnp.zeros((KPAD - KROWS, 640), BF16)
    s_lo[KROWS:KPAD, :] = jnp.zeros((KPAD - KROWS, 640), BF16)
    pl.semaphore_wait(barrier, expected)

    def halo(n, dr, dc):
        return pltpu.make_async_remote_copy(
            src_ref=spectra_ref,
            dst_ref=block_ref.at[1 - dr, 1 - dc],
            send_sem=halo_send.at[n],
            recv_sem=halo_recv.at[n],
            device_id={"inl": inl + dr, "xl": xl + dc},
            device_id_type=MESH,
        )

    for n, (dr, dc) in enumerate(sides):

        @pl.when(exists(dr, dc))
        def _(n=n, dr=dr, dc=dc):
            halo(n, dr, dc).start()

    for dr, dc in sides:

        @pl.when(jnp.logical_not(exists(dr, dc)))
        def _(dr=dr, dc=dc):
            block_ref[1 + dr, 1 + dc] = jnp.zeros((2, 16, LANES), F32)

    omega_copy.wait()
    prepare_weights(omega_ref, taps_ref, band_hi, band_lo)

    own_copy.wait()
    for n, (dr, dc) in enumerate(sides):

        @pl.when(exists(dr, dc))
        def _(n=n, dr=dr, dc=dc):
            halo(n, dr, dc).wait_send()

        @pl.when(exists(-dr, -dc))
        def _(n=n, dr=dr, dc=dc):
            halo(n, dr, dc).wait_recv()

    def sketch_rows(shift, at, width):
        rows = slice(shift * CH, (shift + 1) * CH)
        left_hi = band_hi[rows, :]
        right = s_hi[:, at : at + width]
        return mm(left_hi, right) + mm(band_lo[rows, :], right) + mm(left_hi, s_lo[:, at : at + width])

    def piece(at):
        share = TROWS // n_inl
        return pl.ds(pl.multiple_of(at * share, 8), share)

    def exchange(axis, source, slots, sems):
        me, count = (inl, n_inl) if axis == "inl" else (xl, n_xl)
        send, recv = sems
        pieces = source.shape[0] != slots.shape[1]

        def copy(k):
            peer = lax.rem(me + k, count)
            return pltpu.make_async_remote_copy(
                src_ref=source.at[piece(peer)] if pieces else source,
                dst_ref=slots.at[me],
                send_sem=send.at[k],
                recv_sem=recv.at[k],
                device_id={axis: peer},
                device_id_type=MESH,
            )

        def start():
            for k in range(1, count):
                copy(k).start()
            slots[me] = source[piece(me), :] if pieces else source[...]

        def wait():
            for k in range(1, count):
                copy(k).wait()

        return start, wait

    def summed(slots):
        values = [slots[k] for k in range(slots.shape[0])]
        while len(values) > 1:
            values = [a + b for a, b in zip(values[::2], values[1::2])]
        return values[0]

    gram_xl = exchange("xl", gram_ref, gram_b, (gb_send, gb_recv))
    gram_inl = exchange("inl", gram_part, gram_c, (gc_send, gc_recv))
    scatter_inl = exchange("inl", send_ref, recv_a, (a_send, a_recv))
    across_xl = exchange("xl", part_ref, recv_b, (b_send, b_recv))
    gather_inl = exchange("inl", full_ref, recv_c, (c_send, c_recv))

    stage = pl.loop(0, 1 + jnp.minimum(inl, 0))

    @stage
    def _(_once):
        build_main(block_ref, s_hi, s_lo)
        sums = None
        for shift in range(8):
            value = sketch_rows(shift, LANES, 2 * LANES)
            for half in range(2):
                sketch_ref[pl.ds(8 * half + shift, CH, stride=16), :] = value[
                    :, half * LANES : (half + 1) * LANES
                ]
            high, low = split(value)
            y_hi[shift * CH : (shift + 1) * CH, 128:384] = high
            y_lo[shift * CH : (shift + 1) * CH, 128:384] = low
            term = mm_t(jnp.concatenate([high, low], axis=0), high)
            sums = term if sums is None else sums + term
        sign = jnp.where(lane_iota(1) < HALF, 1.0, -1.0)
        products = sums[:CH] + (sums[CH:] + sums[CH:].T)
        gram = products[:HALF] + roll(products[HALF:], HALF) * sign
        lane = lane_iota(HALF)
        sub = lax.broadcasted_iota(jnp.int32, (HALF, LANES), 0)
        gram = jnp.where(sub >= lane, gram, roll(gram, HALF))
        gram_ref[...] = jnp.where(lane[:32] < HALF, gram[:32], roll(gram[32:], HALF))
        gram_xl[0]()

    @stage
    def _(_once):
        main_hi, main_lo = s_hi[0:KROWS, 128:384], s_lo[0:KROWS, 128:384]
        prod_ref[KROWS : KROWS + 8, :] = jnp.zeros((8, 256), F32)
        total = None
        for pair in range(4):
            rows = slice(pair * 256, (pair + 1) * 256)
            own_hi = y_hi[rows, 128:384]
            prod_ref[0:KROWS, :] = (
                mm_t(main_hi, own_hi) + mm_t(main_lo, own_hi) + mm_t(main_hi, y_lo[rows, 128:384])
            )
            for k in range(2):
                term = prod_ref[2 * pair + k : 2 * pair + k + KROWS, k * LANES : (k + 1) * LANES]
                total = term if total is None else total + term
        prod_ref[0:KROWS, 0:LANES] = total
        first = prod_ref[0 : KROWS // 2, 0:LANES]
        second = prod_ref[KROWS // 2 : KROWS, 0:LANES]
        sign = jnp.where(lane_iota(1) < HALF, 1.0, -1.0)
        moments = roll(second, HALF) + first * sign
        for q in range(KI):
            send_ref[q * 16 : q * 16 + 16, :] = moments[q * WIN : q * WIN + 16]
            send_ref[272 + q : 273 + q, :] = moments[q * WIN + 16 : q * WIN + 17]
        send_ref[289:TROWS, :] = jnp.zeros((TROWS - 289, LANES), F32)
        scatter_inl[0]()

    def outer_rows(shifts):
        side_lane = lane_iota(1)
        keep_up = up.astype(F32)
        keep_down = down.astype(F32)
        keep_side = jnp.where(side_lane % 16 < 8, west.astype(F32), east.astype(F32)) * jnp.where(
            side_lane < 16, keep_up, jnp.where((side_lane >= 48) & (side_lane < 64), keep_down, 1.0)
        )
        keep = jnp.concatenate([jnp.full((1, LANES), keep_down), keep_side], axis=1)
        for shift in shifts:
            rows = slice(shift * CH, (shift + 1) * CH)
            high, low = split(sketch_rows(shift, 0, LANES) * keep_up)
            y_hi[rows, 0:128] = high
            y_lo[rows, 0:128] = low
            high, low = split(sketch_rows(shift, 384, 256) * keep)
            y_hi[rows, 384:640] = high
            y_lo[rows, 384:640] = low

    @stage
    def _(_once):
        build_side(block_ref, s_hi, s_lo)
        outer_rows(range(4))

    @stage
    def _(_once):
        gram_xl[1]()
        gram_part[...] = summed(gram_b)
        gram_inl[0]()

    @stage
    def _(_once):
        outer_rows(range(4, 8))

    @stage
    def _(_once):
        scatter_inl[1]()
        part_ref[...] = summed(recv_a)
        across_xl[0]()

    @stage
    def _(_once):
        gram_inl[1]()
        packed = summed(gram_c)
        packed = jnp.concatenate([packed, roll(packed, HALF)], axis=0)
        flipped = jnp.concatenate([packed, jnp.zeros_like(packed)], axis=0).T[:HALF]
        lane = lane_iota(HALF)
        sub = lax.broadcasted_iota(jnp.int32, (HALF, LANES), 0)
        real = jnp.where(sub >= lane, packed, flipped)
        imag = jnp.where(sub < lane, packed, jnp.where(sub > lane, -flipped, 0.0))
        matrix_ref[...] = jnp.where(lane < HALF, real, roll(imag, HALF))

    @stage
    def _(_once):
        across_xl[1]()
        full_ref[...] = summed(recv_b)
        gather_inl[0]()

    @stage
    def _(_once):
        inverse_ref[...] = invert(matrix_ref[...])

    @stage
    def _(_once):
        gather_inl[1]()
        moments_ref[...] = recv_c[...].reshape(TROWS, LANES)


def spread_kernel(
    n_inl,
    n_xl,
    sketch_ref,
    moments_ref,
    inverse_ref,
    y_hi,
    y_lo,
    sketch_out,
    denoised_ref,
    spread_ref,
    c_hi,
    c_lo,
    out_sem,
):
    inl = lax.axis_index("inl")
    xl = lax.axis_index("xl")
    copy_out = pltpu.make_async_copy(sketch_ref, sketch_out, out_sem)
    copy_out.start()
    sign = jnp.where(lane_iota(1) < HALF, 1.0, -1.0)
    inverse = inverse_ref[...]
    mixing = jnp.concatenate([inverse * sign, roll(inverse, HALF)], axis=0)
    coeffs = mm_exact(moments_ref[...], mixing)

    spread_ref[:, 0:8, :] = jnp.zeros((GROUPS, 8, LANES), F32)
    spread_ref[:, 24:32, :] = jnp.zeros((GROUPS, 8, LANES), F32)
    for x, value in enumerate((coeffs * sign, roll(coeffs, HALF))):
        for q in range(KI):
            spread_ref[x * KI + q, 8:24, :] = value[q * 16 : q * 16 + 16]
            spread_ref[x * KI + q, 24:25, :] = value[272 + q : 273 + q]

    main = None
    edge = None
    for window in range(3):
        for shift in range(8):
            at = 8 + 8 * window - shift
            value = spread_ref[:, at : at + 8, :].reshape(GROUPS * 8, LANES)
            high, low = split(value)
            c_hi[:, shift * LANES : (shift + 1) * LANES] = high
            c_lo[:, shift * LANES : (shift + 1) * LANES] = low
        high, low = c_hi[...], c_lo[...]
        at = (2 - window) * LANES
        y = y_hi[:, at : at + 256]
        term = mm(high, y) + mm(low, y) + mm(high, y_lo[:, at : at + 256])
        main = term if main is None else main + term
        y = y_hi[:, 512:640]
        term = mm(high, y) + mm(low, y) + mm(high, y_lo[:, 512:640])
        term = roll(term, 16 * (window - 2))
        edge = term if edge is None else edge + term

    copy_out.wait()
    lane = lane_iota(8)
    sub = lax.broadcasted_iota(jnp.int32, (8, LANES), 0)
    count_j = counts(xl * LANES, LANES, n_xl * LANES, lane)
    for x in range(2):
        for h in range(2):
            total = None
            for q in range(KI):
                s = q - HW
                rows = slice((x * KI + q) * 8, (x * KI + q) * 8 + 8)
                value = roll(main[rows, h * LANES : (h + 1) * LANES], s)
                if s != 0:
                    outer = roll(edge[rows, :], s - 8 - 16 * h)
                    value = jnp.where(lane < s if s > 0 else lane >= LANES + s, outer, value)
                total = value if total is None else total + value
            count_i = counts(inl * 16 + 8 * h, 16, n_inl * 16, sub)
            denoised_ref[x, 8 * h : 8 * h + 8, :] = total / (count_i * count_j)


def per_device(n_inl, n_xl, spectra, omega):
    vmem = pltpu.VMEM
    dma = pltpu.SemaphoreType.DMA
    here = pl.BlockSpec(memory_space=pltpu.VMEM)
    anywhere = pl.BlockSpec(memory_space=pl.ANY)
    limit = 24 * 1024 * 1024

    share = TROWS // n_inl
    inl_sems = [dma((n_inl,))] * 2
    xl_sems = [dma((n_xl,))] * 2
    results = pl.pallas_call(
        functools.partial(gather_kernel, n_inl, n_xl),
        out_shape=(
            jax.ShapeDtypeStruct((CH * 16, LANES), F32),
            jax.ShapeDtypeStruct((TROWS, LANES), F32),
            jax.ShapeDtypeStruct((HALF, LANES), F32),
            jax.ShapeDtypeStruct((8 * CH, 640), BF16),
            jax.ShapeDtypeStruct((8 * CH, 640), BF16),
        ),
        in_specs=[pl.BlockSpec(memory_space=pltpu.HBM)] * 2,
        out_specs=(here,) * 5,
        scratch_shapes=[
            vmem((3, 3, 2, 16, LANES), F32),
            vmem((2, HALF, KI * KI), F32),
            vmem((CH, TROWS), F32),
            vmem((8 * CH, KPAD), BF16),
            vmem((8 * CH, KPAD), BF16),
            vmem((KPAD, 640), BF16),
            vmem((KPAD, 640), BF16),
            vmem((KROWS + 8, 256), F32),
            vmem((TROWS, LANES), F32),
            vmem((32, LANES), F32),
            vmem((n_xl, 32, LANES), F32),
            vmem((32, LANES), F32),
            vmem((n_inl, 32, LANES), F32),
            vmem((HALF, LANES), F32),
            vmem((n_inl, share, LANES), F32),
            vmem((share, LANES), F32),
            vmem((n_xl, share, LANES), F32),
            vmem((share, LANES), F32),
            vmem((n_inl, share, LANES), F32),
            dma((8,)),
            dma((8,)),
            *inl_sems,
            *xl_sems,
            *inl_sems,
            *xl_sems,
            *inl_sems,
            dma,
            dma,
        ],
        compiler_params=pltpu.CompilerParams(
            collective_id=0, has_side_effects=True, vmem_limit_bytes=limit
        ),
    )(
        pltpu.with_memory_space_constraint(spectra[0], pltpu.HBM),
        pltpu.with_memory_space_constraint(omega.transpose(0, 2, 1), pltpu.HBM),
    )
    sketch, denoised = pl.pallas_call(
        functools.partial(spread_kernel, n_inl, n_xl),
        out_shape=(
            jax.ShapeDtypeStruct((CH * 16, LANES), F32),
            jax.ShapeDtypeStruct((2, 16, LANES), F32),
        ),
        in_specs=[anywhere] + [here] * 4,
        out_specs=(anywhere, here),
        scratch_shapes=[
            vmem((GROUPS, 32, LANES), F32),
            vmem((GROUPS * 8, 8 * LANES), BF16),
            vmem((GROUPS * 8, 8 * LANES), BF16),
            dma,
        ],
        compiler_params=pltpu.CompilerParams(vmem_limit_bytes=limit),
    )(*results)
    return sketch.reshape(1, CH, 16, LANES), denoised[None]


def solution(mesh):
    in_specs = (P("freq", None, "inl", "xl"), P())
    out_specs = (P("freq", None, "inl", "xl"), P("freq", None, "inl", "xl"))
    return jax.shard_map(
        functools.partial(per_device, mesh.shape["inl"], mesh.shape["xl"]),
        mesh=mesh,
        in_specs=in_specs,
        out_specs=out_specs,
        check_vma=False,
    )
```

```python
import functools

import jax
import jax.numpy as jnp
from jax import lax
from jax.experimental import pallas as pl
from jax.experimental.pallas import tpu as pltpu
from jax.sharding import PartitionSpec as P

MESH = pl.DeviceIdType.MESH
F32 = jnp.float32
BF16 = jnp.bfloat16
KI = 17
HW = 8
WIN = 24
GROUPS = 2 * KI
KROWS = GROUPS * WIN
KPAD = 896
TROWS = 384
LANES = 128
CH = 128
HALF = 64


def split(value):
    high = value.astype(BF16)
    return high, (value - high.astype(F32)).astype(BF16)


def mm(a, b):
    return jnp.dot(a, b, preferred_element_type=F32)


def mm_t(a, b):
    return lax.dot_general(a, b, (((1,), (1,)), ((), ())), preferred_element_type=F32)


def roll(value, amount, axis=1):
    size = value.shape[axis]
    amount = amount % size
    return value if amount == 0 else pltpu.roll(value, amount, axis)


def lane_iota(rows, lanes=LANES):
    return lax.broadcasted_iota(jnp.int32, (rows, lanes), 1)


def prepare_weights(omega_ref, taps_ref, band_hi, band_lo):
    taps_ref[:, 256:TROWS] = jnp.zeros((CH, TROWS - 256), F32)
    taps_ref[0:HALF, 0 : KI * KI] = omega_ref[0]
    taps_ref[HALF:CH, 0 : KI * KI] = omega_ref[1]
    tap_t = taps_ref[...]
    turned = jnp.concatenate([-tap_t[HALF:], tap_t[:HALF]], axis=0)
    col = lane_iota(1, KPAD)
    second = col >= KROWS // 2
    inner = jnp.where(second, col - KROWS // 2, col)
    q = (inner * 2731) >> 16
    r = inner - q * WIN
    tap = jnp.where((r < KI) & (col < KROWS), r * KI + q, -1)
    row = lax.broadcasted_iota(jnp.int32, (TROWS, KPAD), 0)
    pick_re = (row == jnp.where(second, -1, tap)).astype(F32).astype(BF16)
    pick_im = (row == jnp.where(second, tap, -1)).astype(F32).astype(BF16)
    re_hi, re_lo = split(tap_t)
    im_hi, im_lo = split(turned)
    wide_hi = mm(re_hi, pick_re) + mm(im_hi, pick_im)
    wide_lo = mm(re_lo, pick_re) + mm(im_lo, pick_im)
    for shift in range(8):
        band_hi[shift * CH : (shift + 1) * CH, :] = roll(wide_hi, shift).astype(BF16)
        band_lo[shift * CH : (shift + 1) * CH, :] = roll(wide_lo, shift).astype(BF16)


def shifted(left, centre, right, s, lane):
    if s == 0:
        return centre
    if s < 0:
        return jnp.where(lane < -s, roll(left, -s), roll(centre, -s))
    return jnp.where(lane >= LANES - s, roll(right, LANES - s), roll(centre, LANES - s))


def plane(block_ref, x, dc):
    return jnp.concatenate([block_ref[dr, dc, x] for dr in range(3)], axis=0)


def build_main(block_ref, s_hi, s_lo):
    lane = lane_iota(48)
    windows = []
    for x in range(2):
        left, centre, right = (plane(block_ref, x, dc) for dc in range(3))
        for q in range(KI):
            windows.append(shifted(left, centre, right, q - HW, lane))
    for k in range(KI):
        first, second = windows[2 * k], windows[2 * k + 1]
        for g in range(4):
            value = jnp.concatenate([first[8 * g : 8 * g + WIN], second[8 * g : 8 * g + WIN]], axis=0)
            high, low = split(value)
            s_hi[48 * k : 48 * k + 48, g * LANES : (g + 1) * LANES] = high
            s_lo[48 * k : 48 * k + 48, g * LANES : (g + 1) * LANES] = low


def build_side(block_ref, s_hi, s_lo):
    lane = lane_iota(48)
    strips = []
    for x in range(2):
        left, centre, right = (plane(block_ref, x, dc) for dc in range(3))
        for q in range(KI):
            inner = roll(centre, 16 - q)
            near = lane < 16 - q
            strip = jnp.where(
                lane < 8,
                jnp.where(near, roll(left, 16 - q), inner),
                jnp.where(near, inner, roll(right, 16 - q)),
            )
            strip = jnp.where(lane < 16, strip, 0.0)
            total = strip[0:WIN]
            for g in range(1, 4):
                total = total + roll(strip[8 * g : 8 * g + WIN], 16 * g)
            strips.append(total)
    for k in range(KI):
        high, low = split(jnp.concatenate([strips[2 * k], strips[2 * k + 1]], axis=0))
        s_hi[48 * k : 48 * k + 48, 512:640] = high
        s_lo[48 * k : 48 * k + 48, 512:640] = low


def invert(matrix):
    shape = (8, LANES)
    lane = lane_iota(8)
    pair = (lane & (HALF - 1)) >> 1
    sub = lax.broadcasted_iota(jnp.int32, shape, 0)
    turn = jnp.where(lane < HALF, -1.0, 1.0)
    tiles = [matrix[8 * v : 8 * v + 8] for v in range(HALF // 8)]

    def fill(value):
        return jnp.broadcast_to(value, shape)

    for k in range(0, HALF, 2):
        v, r = divmod(k, 8)
        row1, row2 = fill(tiles[v][r : r + 1, :]), fill(tiles[v][r + 1 : r + 2, :])
        a, d = fill(row1[:, k : k + 1]), fill(row2[:, k + 1 : k + 2])
        br, bi = fill(row1[:, k + 1 : k + 2]), fill(row1[:, HALF + k + 1 : HALF + k + 2])
        cut = pair == k // 2
        row1 = jnp.where(cut, jnp.where(lane == k, 1.0, 0.0), row1)
        row2 = jnp.where(cut, jnp.where(lane == k + 1, 1.0, 0.0), row2)
        turned1, turned2 = roll(row1, HALF) * turn, roll(row2, HALF) * turn
        p1 = 1.0 / a
        er, ei = br * p1, bi * p1
        p2 = 1.0 / (d - (br * er + bi * ei))
        new2 = p2 * (row2 - (er * row1 - ei * turned1))
        spun2 = p2 * (turned2 - (er * turned1 + ei * row1))
        new1 = p1 * row1 - (er * new2 + ei * spun2)
        spun1 = p1 * turned1 - (er * spun2 - ei * new2)
        after = []
        for w, tile in enumerate(tiles):
            first = fill(tile[:, k : k + 1]) * new1 + fill(tile[:, HALF + k : HALF + k + 1]) * spun1
            second = (
                fill(tile[:, k + 1 : k + 2]) * new2
                + fill(tile[:, HALF + k + 1 : HALF + k + 2]) * spun2
            )
            value = jnp.where(cut, 0.0, tile) - (first + second)
            if w == v:
                value = jnp.where(sub == r, new1, jnp.where(sub == r + 1, new2, value))
            after.append(value)
        tiles = after
    return jnp.concatenate(tiles, axis=0)


def counts(start, length, total, index):
    at = start + index
    return (jnp.minimum(at + HW, total - 1) - jnp.maximum(at - HW, 0) + 1).astype(F32)


def gather_kernel(
    n_inl,
    n_xl,
    spectra_ref,
    omega_hbm,
    sketch_ref,
    moments_ref,
    inverse_ref,
    y_hi,
    y_lo,
    block_ref,
    omega_ref,
    taps_ref,
    band_hi,
    band_lo,
    s_hi,
    s_lo,
    prod_ref,
    send_ref,
    gram_ref,
    gram_b,
    gram_part,
    gram_c,
    matrix_ref,
    recv_a,
    part_ref,
    recv_b,
    full_ref,
    recv_c,
    halo_send,
    halo_recv,
    a_send,
    a_recv,
    b_send,
    b_recv,
    c_send,
    c_recv,
    gb_send,
    gb_recv,
    gc_send,
    gc_recv,
    own_sem,
    omega_sem,
):
    own_copy = pltpu.make_async_copy(spectra_ref, block_ref.at[1, 1], own_sem)
    own_copy.start()
    omega_copy = pltpu.make_async_copy(omega_hbm, omega_ref, omega_sem)
    omega_copy.start()
    inl = lax.axis_index("inl")
    xl = lax.axis_index("xl")
    up, down = inl > 0, inl < n_inl - 1
    west, east = xl > 0, xl < n_xl - 1
    barrier = pltpu.get_barrier_semaphore()
    sides = [(dr, dc) for dr in (-1, 0, 1) for dc in (-1, 0, 1) if (dr, dc) != (0, 0)]

    def exists(dr, dc):
        ok = None
        for step, low, high in ((dr, up, down), (dc, west, east)):
            if step != 0:
                one = low if step < 0 else high
                ok = one if ok is None else ok & one
        return ok

    def greet(axis, steps):
        me, count = (inl, n_inl) if axis == "inl" else (xl, n_xl)
        for k in steps:
            pl.semaphore_signal(
                barrier, inc=1, device_id={axis: lax.rem(me + k, count)}, device_id_type=MESH
            )

    greet("inl", sorted({1, n_inl - 1}))
    greet("xl", sorted({1, n_xl - 1}))
    expected = n_inl - 1 + n_xl - 1
    for dr, dc in sides:
        if dr != 0 and dc != 0:
            there = exists(dr, dc)
            expected = expected + there.astype(jnp.int32)

            @pl.when(there)
            def _(dr=dr, dc=dc):
                pl.semaphore_signal(
                    barrier, inc=1, device_id={"inl": inl + dr, "xl": xl + dc}, device_id_type=MESH
                )

    greet("inl", range(2, n_inl - 1))
    greet("xl", range(2, n_xl - 1))
    s_hi[KROWS:KPAD, :] = jnp.zeros((KPAD - KROWS, 640), BF16)
    s_lo[KROWS:KPAD, :] = jnp.zeros((KPAD - KROWS, 640), BF16)
    pl.semaphore_wait(barrier, expected)

    def halo(n, dr, dc):
        return pltpu.make_async_remote_copy(
            src_ref=spectra_ref,
            dst_ref=block_ref.at[1 - dr, 1 - dc],
            send_sem=halo_send.at[n],
            recv_sem=halo_recv.at[n],
            device_id={"inl": inl + dr, "xl": xl + dc},
            device_id_type=MESH,
        )

    for n, (dr, dc) in enumerate(sides):

        @pl.when(exists(dr, dc))
        def _(n=n, dr=dr, dc=dc):
            halo(n, dr, dc).start()

    for dr, dc in sides:

        @pl.when(jnp.logical_not(exists(dr, dc)))
        def _(dr=dr, dc=dc):
            block_ref[1 + dr, 1 + dc] = jnp.zeros((2, 16, LANES), F32)

    omega_copy.wait()
    prepare_weights(omega_ref, taps_ref, band_hi, band_lo)

    own_copy.wait()
    for n, (dr, dc) in enumerate(sides):

        @pl.when(exists(dr, dc))
        def _(n=n, dr=dr, dc=dc):
            halo(n, dr, dc).wait_send()

        @pl.when(exists(-dr, -dc))
        def _(n=n, dr=dr, dc=dc):
            halo(n, dr, dc).wait_recv()

    def sketch_rows(shift, at, width):
        rows = slice(shift * CH, (shift + 1) * CH)
        left_hi = band_hi[rows, :]
        right = s_hi[:, at : at + width]
        return mm(left_hi, right) + mm(band_lo[rows, :], right) + mm(left_hi, s_lo[:, at : at + width])

    def piece(at):
        share = TROWS // n_inl
        return pl.ds(pl.multiple_of(at * share, 8), share)

    def exchange(axis, source, slots, sems):
        me, count = (inl, n_inl) if axis == "inl" else (xl, n_xl)
        send, recv = sems
        pieces = source.shape[0] != slots.shape[1]

        def copy(k):
            peer = lax.rem(me + k, count)
            return pltpu.make_async_remote_copy(
                src_ref=source.at[piece(peer)] if pieces else source,
                dst_ref=slots.at[me],
                send_sem=send.at[k],
                recv_sem=recv.at[k],
                device_id={axis: peer},
                device_id_type=MESH,
            )

        def start():
            for k in range(1, count):
                copy(k).start()
            slots[me] = source[piece(me), :] if pieces else source[...]

        def wait():
            for k in range(1, count):
                copy(k).wait()

        return start, wait

    def summed(slots):
        values = [slots[k] for k in range(slots.shape[0])]
        while len(values) > 1:
            values = [a + b for a, b in zip(values[::2], values[1::2])]
        return values[0]

    gram_xl = exchange("xl", gram_ref, gram_b, (gb_send, gb_recv))
    gram_inl = exchange("inl", gram_part, gram_c, (gc_send, gc_recv))
    scatter_inl = exchange("inl", send_ref, recv_a, (a_send, a_recv))
    across_xl = exchange("xl", part_ref, recv_b, (b_send, b_recv))
    gather_inl = exchange("inl", full_ref, recv_c, (c_send, c_recv))

    stage = pl.loop(0, 1 + jnp.minimum(inl, 0))

    @stage
    def _(_once):
        build_main(block_ref, s_hi, s_lo)
        sums = None
        for shift in range(8):
            value = sketch_rows(shift, LANES, 2 * LANES)
            for half in range(2):
                sketch_ref[pl.ds(8 * half + shift, CH, stride=16), :] = value[
                    :, half * LANES : (half + 1) * LANES
                ]
            high, low = split(value)
            y_hi[shift * CH : (shift + 1) * CH, 128:384] = high
            y_lo[shift * CH : (shift + 1) * CH, 128:384] = low
            term = mm_t(jnp.concatenate([high, low], axis=0), high)
            sums = term if sums is None else sums + term
        sign = jnp.where(lane_iota(1) < HALF, 1.0, -1.0)
        products = sums[:CH] + (sums[CH:] + sums[CH:].T)
        gram = products[:HALF] + roll(products[HALF:], HALF) * sign
        lane = lane_iota(HALF)
        sub = lax.broadcasted_iota(jnp.int32, (HALF, LANES), 0)
        gram = jnp.where(sub >= lane, gram, roll(gram, HALF))
        gram_ref[...] = jnp.where(lane[:32] < HALF, gram[:32], roll(gram[32:], HALF))
        gram_xl[0]()

    @stage
    def _(_once):
        main_hi, main_lo = s_hi[0:KROWS, 128:384], s_lo[0:KROWS, 128:384]
        prod_ref[KROWS : KROWS + 8, :] = jnp.zeros((8, 256), F32)
        total = None
        for pair in range(4):
            rows = slice(pair * 256, (pair + 1) * 256)
            own_hi = y_hi[rows, 128:384]
            prod_ref[0:KROWS, :] = (
                mm_t(main_hi, own_hi) + mm_t(main_lo, own_hi) + mm_t(main_hi, y_lo[rows, 128:384])
            )
            for k in range(2):
                term = prod_ref[2 * pair + k : 2 * pair + k + KROWS, k * LANES : (k + 1) * LANES]
                total = term if total is None else total + term
        prod_ref[0:KROWS, 0:LANES] = total
        first = prod_ref[0 : KROWS // 2, 0:LANES]
        second = prod_ref[KROWS // 2 : KROWS, 0:LANES]
        sign = jnp.where(lane_iota(1) < HALF, 1.0, -1.0)
        moments = roll(second, HALF) + first * sign
        for q in range(KI):
            send_ref[q * 16 : q * 16 + 16, :] = moments[q * WIN : q * WIN + 16]
            send_ref[272 + q : 273 + q, :] = moments[q * WIN + 16 : q * WIN + 17]
        send_ref[289:TROWS, :] = jnp.zeros((TROWS - 289, LANES), F32)
        scatter_inl[0]()

    def outer_rows(shifts):
        side_lane = lane_iota(1)
        keep_up = up.astype(F32)
        keep_down = down.astype(F32)
        keep_side = jnp.where(side_lane % 16 < 8, west.astype(F32), east.astype(F32)) * jnp.where(
            side_lane < 16, keep_up, jnp.where((side_lane >= 48) & (side_lane < 64), keep_down, 1.0)
        )
        keep = jnp.concatenate([jnp.full((1, LANES), keep_down), keep_side], axis=1)
        for shift in shifts:
            rows = slice(shift * CH, (shift + 1) * CH)
            high, low = split(sketch_rows(shift, 0, LANES) * keep_up)
            y_hi[rows, 0:128] = high
            y_lo[rows, 0:128] = low
            high, low = split(sketch_rows(shift, 384, 256) * keep)
            y_hi[rows, 384:512] = high[:, :LANES]
            y_lo[rows, 384:512] = low[:, :LANES]
            rest = roll(low[:, LANES:].astype(F32), HALF)
            y_hi[rows, 512:640] = jnp.where(side_lane < HALF, high[:, LANES:].astype(F32), rest).astype(BF16)

    @stage
    def _(_once):
        build_side(block_ref, s_hi, s_lo)
        outer_rows(range(4))

    @stage
    def _(_once):
        gram_xl[1]()
        gram_part[...] = summed(gram_b)
        gram_inl[0]()

    @stage
    def _(_once):
        outer_rows(range(4, 8))

    @stage
    def _(_once):
        scatter_inl[1]()
        part_ref[...] = summed(recv_a)
        across_xl[0]()

    @stage
    def _(_once):
        gram_inl[1]()
        packed = summed(gram_c)
        packed = jnp.concatenate([packed, roll(packed, HALF)], axis=0)
        flipped = jnp.concatenate([packed, jnp.zeros_like(packed)], axis=0).T[:HALF]
        lane = lane_iota(HALF)
        sub = lax.broadcasted_iota(jnp.int32, (HALF, LANES), 0)
        real = jnp.where(sub >= lane, packed, flipped)
        imag = jnp.where(sub < lane, packed, jnp.where(sub > lane, -flipped, 0.0))
        matrix_ref[...] = jnp.where(lane < HALF, real, roll(imag, HALF))

    @stage
    def _(_once):
        across_xl[1]()
        full_ref[...] = summed(recv_b)
        gather_inl[0]()

    @stage
    def _(_once):
        inverse_ref[...] = invert(matrix_ref[...])

    @stage
    def _(_once):
        gather_inl[1]()
        moments_ref[...] = recv_c[...].reshape(TROWS, LANES)


def spread_kernel(
    n_inl,
    n_xl,
    sketch_ref,
    moments_ref,
    inverse_ref,
    y_hi,
    y_lo,
    sketch_out,
    denoised_ref,
    spread_ref,
    c_both,
    out_sem,
):
    inl = lax.axis_index("inl")
    xl = lax.axis_index("xl")
    copy_out = pltpu.make_async_copy(sketch_ref, sketch_out, out_sem)
    copy_out.start()
    sign = jnp.where(lane_iota(1) < HALF, 1.0, -1.0)
    inverse = inverse_ref[...]
    mixing = jnp.concatenate([inverse * sign, roll(inverse, HALF)], axis=0)
    mixing_hi, mixing_lo = split(mixing)
    high, low = split(moments_ref[...])
    coeffs = mm(high, mixing_hi) + mm(low, mixing_hi) + mm(high, mixing_lo)

    spread_ref[:, 0:8, :] = jnp.zeros((GROUPS, 8, LANES), F32)
    spread_ref[:, 24:32, :] = jnp.zeros((GROUPS, 8, LANES), F32)
    for x, value in enumerate((coeffs * sign, roll(coeffs, HALF))):
        for q in range(KI):
            spread_ref[x * KI + q, 8:24, :] = value[q * 16 : q * 16 + 16]
            spread_ref[x * KI + q, 24:25, :] = value[272 + q : 273 + q]

    size = GROUPS * 8
    main = None
    edge = None
    for window in range(3):
        for shift in range(8):
            at = 8 + 8 * window - shift
            value = spread_ref[:, at : at + 8, :].reshape(size, LANES)
            high, low = split(value)
            c_both[0:size, shift * LANES : (shift + 1) * LANES] = high
            c_both[size : 2 * size, shift * LANES : (shift + 1) * LANES] = low
        both = c_both[...]
        at = (2 - window) * LANES
        term = mm(both, y_hi[:, at : at + 256])
        term = term[:size] + term[size:] + mm(both[:size], y_lo[:, at : at + 256])
        main = term if main is None else main + term
        term = mm(both, y_hi[:, 512:640])
        term = term[:size] + roll(term[:size], HALF) + term[size:]
        term = roll(term, 16 * (window - 2))
        edge = term if edge is None else edge + term

    copy_out.wait()
    lane = lane_iota(8)
    sub = lax.broadcasted_iota(jnp.int32, (8, LANES), 0)
    count_j = counts(xl * LANES, LANES, n_xl * LANES, lane)
    for x in range(2):
        for h in range(2):
            total = None
            for q in range(KI):
                s = q - HW
                rows = slice((x * KI + q) * 8, (x * KI + q) * 8 + 8)
                value = roll(main[rows, h * LANES : (h + 1) * LANES], s)
                if s != 0:
                    outer = roll(edge[rows, :], s - 8 - 16 * h)
                    value = jnp.where(lane < s if s > 0 else lane >= LANES + s, outer, value)
                total = value if total is None else total + value
            count_i = counts(inl * 16 + 8 * h, 16, n_inl * 16, sub)
            denoised_ref[x, 8 * h : 8 * h + 8, :] = total / (count_i * count_j)


def per_device(n_inl, n_xl, spectra, omega):
    vmem = pltpu.VMEM
    dma = pltpu.SemaphoreType.DMA
    here = pl.BlockSpec(memory_space=pltpu.VMEM)
    anywhere = pl.BlockSpec(memory_space=pl.ANY)
    limit = 24 * 1024 * 1024

    share = TROWS // n_inl
    inl_sems = [dma((n_inl,))] * 2
    xl_sems = [dma((n_xl,))] * 2
    results = pl.pallas_call(
        functools.partial(gather_kernel, n_inl, n_xl),
        out_shape=(
            jax.ShapeDtypeStruct((CH * 16, LANES), F32),
            jax.ShapeDtypeStruct((TROWS, LANES), F32),
            jax.ShapeDtypeStruct((HALF, LANES), F32),
            jax.ShapeDtypeStruct((8 * CH, 640), BF16),
            jax.ShapeDtypeStruct((8 * CH, 512), BF16),
        ),
        in_specs=[pl.BlockSpec(memory_space=pltpu.HBM)] * 2,
        out_specs=(here,) * 5,
        scratch_shapes=[
            vmem((3, 3, 2, 16, LANES), F32),
            vmem((2, HALF, KI * KI), F32),
            vmem((CH, TROWS), F32),
            vmem((8 * CH, KPAD), BF16),
            vmem((8 * CH, KPAD), BF16),
            vmem((KPAD, 640), BF16),
            vmem((KPAD, 640), BF16),
            vmem((KROWS + 8, 256), F32),
            vmem((TROWS, LANES), F32),
            vmem((32, LANES), F32),
            vmem((n_xl, 32, LANES), F32),
            vmem((32, LANES), F32),
            vmem((n_inl, 32, LANES), F32),
            vmem((HALF, LANES), F32),
            vmem((n_inl, share, LANES), F32),
            vmem((share, LANES), F32),
            vmem((n_xl, share, LANES), F32),
            vmem((share, LANES), F32),
            vmem((n_inl, share, LANES), F32),
            dma((8,)),
            dma((8,)),
            *inl_sems,
            *xl_sems,
            *inl_sems,
            *xl_sems,
            *inl_sems,
            dma,
            dma,
        ],
        compiler_params=pltpu.CompilerParams(
            collective_id=0, has_side_effects=True, vmem_limit_bytes=limit
        ),
    )(
        pltpu.with_memory_space_constraint(spectra[0], pltpu.HBM),
        pltpu.with_memory_space_constraint(omega.transpose(0, 2, 1), pltpu.HBM),
    )
    sketch, denoised = pl.pallas_call(
        functools.partial(spread_kernel, n_inl, n_xl),
        out_shape=(
            jax.ShapeDtypeStruct((CH * 16, LANES), F32),
            jax.ShapeDtypeStruct((2, 16, LANES), F32),
        ),
        in_specs=[anywhere] + [here] * 4,
        out_specs=(anywhere, here),
        scratch_shapes=[
            vmem((GROUPS, 32, LANES), F32),
            vmem((2 * GROUPS * 8, 8 * LANES), BF16),
            dma,
        ],
        compiler_params=pltpu.CompilerParams(vmem_limit_bytes=limit),
    )(*results)
    return sketch.reshape(1, CH, 16, LANES), denoised[None]


def solution(mesh):
    in_specs = (P("freq", None, "inl", "xl"), P())
    out_specs = (P("freq", None, "inl", "xl"), P("freq", None, "inl", "xl"))
    return jax.shard_map(
        functools.partial(per_device, mesh.shape["inl"], mesh.shape["xl"]),
        mesh=mesh,
        in_specs=in_specs,
        out_specs=out_specs,
        check_vma=False,
    )
```

```python
import functools

import jax
import jax.numpy as jnp
from jax import lax
from jax.experimental import pallas as pl
from jax.experimental.pallas import tpu as pltpu
from jax.sharding import PartitionSpec as P

MESH = pl.DeviceIdType.MESH
F32 = jnp.float32
BF16 = jnp.bfloat16
KI = 17
HW = 8
WIN = 24
GROUPS = 2 * KI
KROWS = GROUPS * WIN
KPAD = 896
TROWS = 384
LANES = 128
CH = 128
HALF = 64


def split(value):
    high = value.astype(BF16)
    return high, (value - high.astype(F32)).astype(BF16)


def mm(a, b):
    return jnp.dot(a, b, preferred_element_type=F32)


def mm_t(a, b):
    return lax.dot_general(a, b, (((1,), (1,)), ((), ())), preferred_element_type=F32)


def roll(value, amount, axis=1):
    size = value.shape[axis]
    amount = amount % size
    return value if amount == 0 else pltpu.roll(value, amount, axis)


def lane_iota(rows, lanes=LANES):
    return lax.broadcasted_iota(jnp.int32, (rows, lanes), 1)


def prepare_weights(omega_ref, taps_ref, band_hi, band_lo):
    taps_ref[:, 256:TROWS] = jnp.zeros((CH, TROWS - 256), F32)
    taps_ref[0:HALF, 0 : KI * KI] = omega_ref[0]
    taps_ref[HALF:CH, 0 : KI * KI] = omega_ref[1]
    tap_t = taps_ref[...]
    turned = jnp.concatenate([-tap_t[HALF:], tap_t[:HALF]], axis=0)
    col = lane_iota(1, KPAD)
    second = col >= KROWS // 2
    inner = jnp.where(second, col - KROWS // 2, col)
    q = (inner * 2731) >> 16
    r = inner - q * WIN
    tap = jnp.where((r < KI) & (col < KROWS), r * KI + q, -1)
    row = lax.broadcasted_iota(jnp.int32, (TROWS, KPAD), 0)
    pick_re = (row == jnp.where(second, -1, tap)).astype(F32).astype(BF16)
    pick_im = (row == jnp.where(second, tap, -1)).astype(F32).astype(BF16)
    re_hi, re_lo = split(tap_t)
    im_hi, im_lo = split(turned)
    wide_hi = mm(re_hi, pick_re) + mm(im_hi, pick_im)
    wide_lo = mm(re_lo, pick_re) + mm(im_lo, pick_im)
    for shift in range(8):
        band_hi[shift * CH : (shift + 1) * CH, :] = roll(wide_hi, shift).astype(BF16)
        band_lo[shift * CH : (shift + 1) * CH, :] = roll(wide_lo, shift).astype(BF16)


def shifted(left, centre, right, s, lane):
    if s == 0:
        return centre
    if s < 0:
        return jnp.where(lane < -s, roll(left, -s), roll(centre, -s))
    return jnp.where(lane >= LANES - s, roll(right, LANES - s), roll(centre, LANES - s))


def plane(block_ref, x, dc):
    return jnp.concatenate([block_ref[dr, dc, x] for dr in range(3)], axis=0)


def build_main(block_ref, s_hi, s_lo):
    lane = lane_iota(48)
    windows = []
    for x in range(2):
        left, centre, right = (plane(block_ref, x, dc) for dc in range(3))
        for q in range(KI):
            windows.append(shifted(left, centre, right, q - HW, lane))
    for k in range(KI):
        first, second = windows[2 * k], windows[2 * k + 1]
        for g in range(4):
            value = jnp.concatenate([first[8 * g : 8 * g + WIN], second[8 * g : 8 * g + WIN]], axis=0)
            high, low = split(value)
            s_hi[48 * k : 48 * k + 48, g * LANES : (g + 1) * LANES] = high
            s_lo[48 * k : 48 * k + 48, g * LANES : (g + 1) * LANES] = low


def build_side(block_ref, s_hi, s_lo):
    lane = lane_iota(48)
    strips = []
    for x in range(2):
        left, centre, right = (plane(block_ref, x, dc) for dc in range(3))
        for q in range(KI):
            inner = roll(centre, 16 - q)
            near = lane < 16 - q
            strip = jnp.where(
                lane < 8,
                jnp.where(near, roll(left, 16 - q), inner),
                jnp.where(near, inner, roll(right, 16 - q)),
            )
            strip = jnp.where(lane < 16, strip, 0.0)
            total = strip[0:WIN]
            for g in range(1, 4):
                total = total + roll(strip[8 * g : 8 * g + WIN], 16 * g)
            strips.append(total)
    for k in range(KI):
        high, low = split(jnp.concatenate([strips[2 * k], strips[2 * k + 1]], axis=0))
        s_hi[48 * k : 48 * k + 48, 512:640] = high
        s_lo[48 * k : 48 * k + 48, 512:640] = low


def invert(matrix):
    shape = (8, LANES)
    lane = lane_iota(8)
    pair = (lane & (HALF - 1)) >> 1
    sub = lax.broadcasted_iota(jnp.int32, shape, 0)
    turn = jnp.where(lane < HALF, -1.0, 1.0)
    tiles = [matrix[8 * v : 8 * v + 8] for v in range(HALF // 8)]

    def fill(value):
        return jnp.broadcast_to(value, shape)

    for k in range(0, HALF, 2):
        v, r = divmod(k, 8)
        row1, row2 = fill(tiles[v][r : r + 1, :]), fill(tiles[v][r + 1 : r + 2, :])
        a, d = fill(row1[:, k : k + 1]), fill(row2[:, k + 1 : k + 2])
        br, bi = fill(row1[:, k + 1 : k + 2]), fill(row1[:, HALF + k + 1 : HALF + k + 2])
        cut = pair == k // 2
        row1 = jnp.where(cut, jnp.where(lane == k, 1.0, 0.0), row1)
        row2 = jnp.where(cut, jnp.where(lane == k + 1, 1.0, 0.0), row2)
        turned1, turned2 = roll(row1, HALF) * turn, roll(row2, HALF) * turn
        p1 = 1.0 / a
        er, ei = br * p1, bi * p1
        p2 = 1.0 / (d - (br * er + bi * ei))
        new2 = p2 * (row2 - (er * row1 - ei * turned1))
        spun2 = p2 * (turned2 - (er * turned1 + ei * row1))
        new1 = p1 * row1 - (er * new2 + ei * spun2)
        spun1 = p1 * turned1 - (er * spun2 - ei * new2)
        after = []
        for w, tile in enumerate(tiles):
            first = fill(tile[:, k : k + 1]) * new1 + fill(tile[:, HALF + k : HALF + k + 1]) * spun1
            second = (
                fill(tile[:, k + 1 : k + 2]) * new2
                + fill(tile[:, HALF + k + 1 : HALF + k + 2]) * spun2
            )
            value = jnp.where(cut, 0.0, tile) - (first + second)
            if w == v:
                value = jnp.where(sub == r, new1, jnp.where(sub == r + 1, new2, value))
            after.append(value)
        tiles = after
    return jnp.concatenate(tiles, axis=0)


def counts(start, length, total, index):
    at = start + index
    return (jnp.minimum(at + HW, total - 1) - jnp.maximum(at - HW, 0) + 1).astype(F32)


def gather_kernel(
    n_inl,
    n_xl,
    spectra_ref,
    omega_hbm,
    sketch_ref,
    moments_ref,
    inverse_ref,
    y_hi,
    y_lo,
    block_ref,
    omega_ref,
    taps_ref,
    band_hi,
    band_lo,
    s_hi,
    s_lo,
    prod_ref,
    send_ref,
    gram_ref,
    gram_b,
    gram_part,
    gram_c,
    matrix_ref,
    recv_a,
    part_ref,
    recv_b,
    full_ref,
    recv_c,
    halo_send,
    halo_recv,
    a_send,
    a_recv,
    b_send,
    b_recv,
    c_send,
    c_recv,
    gb_send,
    gb_recv,
    gc_send,
    gc_recv,
    own_sem,
    omega_sem,
):
    own_copy = pltpu.make_async_copy(spectra_ref, block_ref.at[1, 1], own_sem)
    own_copy.start()
    omega_copy = pltpu.make_async_copy(omega_hbm, omega_ref, omega_sem)
    omega_copy.start()
    inl = lax.axis_index("inl")
    xl = lax.axis_index("xl")
    up, down = inl > 0, inl < n_inl - 1
    west, east = xl > 0, xl < n_xl - 1
    barrier = pltpu.get_barrier_semaphore()
    sides = [(-1, -1), (-1, 1), (1, -1), (1, 1), (-1, 0), (1, 0), (0, -1), (0, 1)]

    def exists(dr, dc):
        ok = None
        for step, low, high in ((dr, up, down), (dc, west, east)):
            if step != 0:
                one = low if step < 0 else high
                ok = one if ok is None else ok & one
        return ok

    def greet(axis, steps):
        me, count = (inl, n_inl) if axis == "inl" else (xl, n_xl)
        for k in steps:
            pl.semaphore_signal(
                barrier, inc=1, device_id={axis: lax.rem(me + k, count)}, device_id_type=MESH
            )

    greet("inl", sorted({1, n_inl - 1}))
    greet("xl", sorted({1, n_xl - 1}))
    expected = n_inl - 1 + n_xl - 1
    for dr, dc in sides:
        if dr != 0 and dc != 0:
            there = exists(dr, dc)
            expected = expected + there.astype(jnp.int32)

            @pl.when(there)
            def _(dr=dr, dc=dc):
                pl.semaphore_signal(
                    barrier, inc=1, device_id={"inl": inl + dr, "xl": xl + dc}, device_id_type=MESH
                )

    greet("inl", range(2, n_inl - 1))
    greet("xl", range(2, n_xl - 1))
    s_hi[KROWS:KPAD, :] = jnp.zeros((KPAD - KROWS, 640), BF16)
    s_lo[KROWS:KPAD, :] = jnp.zeros((KPAD - KROWS, 640), BF16)
    pl.semaphore_wait(barrier, expected)

    def halo(n, dr, dc):
        return pltpu.make_async_remote_copy(
            src_ref=spectra_ref,
            dst_ref=block_ref.at[1 - dr, 1 - dc],
            send_sem=halo_send.at[n],
            recv_sem=halo_recv.at[n],
            device_id={"inl": inl + dr, "xl": xl + dc},
            device_id_type=MESH,
        )

    for n, (dr, dc) in enumerate(sides):

        @pl.when(exists(dr, dc))
        def _(n=n, dr=dr, dc=dc):
            halo(n, dr, dc).start()

    for dr, dc in sides:

        @pl.when(jnp.logical_not(exists(dr, dc)))
        def _(dr=dr, dc=dc):
            block_ref[1 + dr, 1 + dc] = jnp.zeros((2, 16, LANES), F32)

    omega_copy.wait()
    prepare_weights(omega_ref, taps_ref, band_hi, band_lo)

    own_copy.wait()
    for n, (dr, dc) in enumerate(sides):

        @pl.when(exists(dr, dc))
        def _(n=n, dr=dr, dc=dc):
            halo(n, dr, dc).wait_send()

        @pl.when(exists(-dr, -dc))
        def _(n=n, dr=dr, dc=dc):
            halo(n, dr, dc).wait_recv()

    def sketch_rows(shift, at, width):
        rows = slice(shift * CH, (shift + 1) * CH)
        left_hi = band_hi[rows, :]
        right = s_hi[:, at : at + width]
        return mm(left_hi, right) + mm(band_lo[rows, :], right) + mm(left_hi, s_lo[:, at : at + width])

    def piece(at):
        share = TROWS // n_inl
        return pl.ds(pl.multiple_of(at * share, 8), share)

    def exchange(axis, source, slots, sems):
        me, count = (inl, n_inl) if axis == "inl" else (xl, n_xl)
        send, recv = sems
        pieces = source.shape[0] != slots.shape[1]

        def copy(k):
            peer = lax.rem(me + k, count)
            return pltpu.make_async_remote_copy(
                src_ref=source.at[piece(peer)] if pieces else source,
                dst_ref=slots.at[me],
                send_sem=send.at[k],
                recv_sem=recv.at[k],
                device_id={axis: peer},
                device_id_type=MESH,
            )

        def hops(k):
            if axis == "xl":
                return min(k, count - k)
            return min(k // 4, count // 4 - k // 4) + min(k % 4, 4 - k % 4)

        far_first = sorted(range(1, count), key=hops, reverse=True)

        def start():
            for k in far_first:
                copy(k).start()
            slots[me] = source[piece(me), :] if pieces else source[...]

        def wait():
            for k in range(1, count):
                copy(k).wait()

        return start, wait

    def summed(slots):
        values = [slots[k] for k in range(slots.shape[0])]
        while len(values) > 1:
            values = [a + b for a, b in zip(values[::2], values[1::2])]
        return values[0]

    gram_xl = exchange("xl", gram_ref, gram_b, (gb_send, gb_recv))
    gram_inl = exchange("inl", gram_part, gram_c, (gc_send, gc_recv))
    scatter_inl = exchange("inl", send_ref, recv_a, (a_send, a_recv))
    across_xl = exchange("xl", part_ref, recv_b, (b_send, b_recv))
    gather_inl = exchange("inl", full_ref, recv_c, (c_send, c_recv))

    stage = pl.loop(0, 1 + jnp.minimum(inl, 0))

    @stage
    def _(_once):
        build_main(block_ref, s_hi, s_lo)
        sums = None
        for shift in range(8):
            value = sketch_rows(shift, LANES, 2 * LANES)
            for half in range(2):
                sketch_ref[pl.ds(8 * half + shift, CH, stride=16), :] = value[
                    :, half * LANES : (half + 1) * LANES
                ]
            high, low = split(value)
            y_hi[shift * CH : (shift + 1) * CH, 128:384] = high
            y_lo[shift * CH : (shift + 1) * CH, 128:384] = low
            term = mm_t(jnp.concatenate([high, low], axis=0), high)
            sums = term if sums is None else sums + term
        sign = jnp.where(lane_iota(1) < HALF, 1.0, -1.0)
        products = sums[:CH] + (sums[CH:] + sums[CH:].T)
        gram = products[:HALF] + roll(products[HALF:], HALF) * sign
        lane = lane_iota(HALF)
        sub = lax.broadcasted_iota(jnp.int32, (HALF, LANES), 0)
        gram = jnp.where(sub >= lane, gram, roll(gram, HALF))
        gram_ref[...] = jnp.where(lane[:32] < HALF, gram[:32], roll(gram[32:], HALF))
        gram_xl[0]()

    @stage
    def _(_once):
        main_hi, main_lo = s_hi[0:KROWS, 128:384], s_lo[0:KROWS, 128:384]
        prod_ref[KROWS : KROWS + 8, :] = jnp.zeros((8, 256), F32)
        total = None
        for pair in range(4):
            rows = slice(pair * 256, (pair + 1) * 256)
            own_hi = y_hi[rows, 128:384]
            prod_ref[0:KROWS, :] = (
                mm_t(main_hi, own_hi) + mm_t(main_lo, own_hi) + mm_t(main_hi, y_lo[rows, 128:384])
            )
            for k in range(2):
                term = prod_ref[2 * pair + k : 2 * pair + k + KROWS, k * LANES : (k + 1) * LANES]
                total = term if total is None else total + term
        prod_ref[0:KROWS, 0:LANES] = total
        first = prod_ref[0 : KROWS // 2, 0:LANES]
        second = prod_ref[KROWS // 2 : KROWS, 0:LANES]
        sign = jnp.where(lane_iota(1) < HALF, 1.0, -1.0)
        moments = roll(second, HALF) + first * sign
        for q in range(KI):
            send_ref[q * 16 : q * 16 + 16, :] = moments[q * WIN : q * WIN + 16]
            send_ref[272 + q : 273 + q, :] = moments[q * WIN + 16 : q * WIN + 17]
        send_ref[289:TROWS, :] = jnp.zeros((TROWS - 289, LANES), F32)
        scatter_inl[0]()

    def outer_rows(shifts):
        side_lane = lane_iota(1)
        keep_up = up.astype(F32)
        keep_down = down.astype(F32)
        keep_side = jnp.where(side_lane % 16 < 8, west.astype(F32), east.astype(F32)) * jnp.where(
            side_lane < 16, keep_up, jnp.where((side_lane >= 48) & (side_lane < 64), keep_down, 1.0)
        )
        keep = jnp.concatenate([jnp.full((1, LANES), keep_down), keep_side], axis=1)
        for shift in shifts:
            rows = slice(shift * CH, (shift + 1) * CH)
            high, low = split(sketch_rows(shift, 0, LANES) * keep_up)
            y_hi[rows, 0:128] = high
            y_lo[rows, 0:128] = low
            high, low = split(sketch_rows(shift, 384, 256) * keep)
            y_hi[rows, 384:512] = high[:, :LANES]
            y_lo[rows, 384:512] = low[:, :LANES]
            rest = roll(low[:, LANES:].astype(F32), HALF)
            y_hi[rows, 512:640] = jnp.where(side_lane < HALF, high[:, LANES:].astype(F32), rest).astype(BF16)

    @stage
    def _(_once):
        build_side(block_ref, s_hi, s_lo)
        outer_rows(range(4))

    @stage
    def _(_once):
        gram_xl[1]()
        gram_part[...] = summed(gram_b)
        gram_inl[0]()

    @stage
    def _(_once):
        scatter_inl[1]()
        part_ref[...] = summed(recv_a)
        across_xl[0]()

    @stage
    def _(_once):
        outer_rows(range(4, 8))

    @stage
    def _(_once):
        gram_inl[1]()
        packed = summed(gram_c)
        packed = jnp.concatenate([packed, roll(packed, HALF)], axis=0)
        flipped = jnp.concatenate([packed, jnp.zeros_like(packed)], axis=0).T[:HALF]
        lane = lane_iota(HALF)
        sub = lax.broadcasted_iota(jnp.int32, (HALF, LANES), 0)
        real = jnp.where(sub >= lane, packed, flipped)
        imag = jnp.where(sub < lane, packed, jnp.where(sub > lane, -flipped, 0.0))
        matrix_ref[...] = jnp.where(lane < HALF, real, roll(imag, HALF))

    @stage
    def _(_once):
        across_xl[1]()
        full_ref[...] = summed(recv_b)
        gather_inl[0]()

    @stage
    def _(_once):
        inverse_ref[...] = invert(matrix_ref[...])

    @stage
    def _(_once):
        gather_inl[1]()
        moments_ref[...] = recv_c[...].reshape(TROWS, LANES)


def spread_kernel(
    n_inl,
    n_xl,
    sketch_ref,
    moments_ref,
    inverse_ref,
    y_hi,
    y_lo,
    sketch_out,
    denoised_ref,
    spread_ref,
    c_both,
    out_sem,
):
    inl = lax.axis_index("inl")
    xl = lax.axis_index("xl")
    copy_out = pltpu.make_async_copy(sketch_ref, sketch_out, out_sem)
    copy_out.start()
    sign = jnp.where(lane_iota(1) < HALF, 1.0, -1.0)
    inverse = inverse_ref[...]
    mixing = jnp.concatenate([inverse * sign, roll(inverse, HALF)], axis=0)
    mixing_hi, mixing_lo = split(mixing)
    high, low = split(moments_ref[...])
    coeffs = mm(high, mixing_hi) + mm(low, mixing_hi) + mm(high, mixing_lo)

    spread_ref[:, 0:8, :] = jnp.zeros((GROUPS, 8, LANES), F32)
    spread_ref[:, 24:32, :] = jnp.zeros((GROUPS, 8, LANES), F32)
    for x, value in enumerate((coeffs * sign, roll(coeffs, HALF))):
        for q in range(KI):
            spread_ref[x * KI + q, 8:24, :] = value[q * 16 : q * 16 + 16]
            spread_ref[x * KI + q, 24:25, :] = value[272 + q : 273 + q]

    size = GROUPS * 8
    main = None
    edge = None
    for window in range(3):
        for shift in range(8):
            at = 8 + 8 * window - shift
            value = spread_ref[:, at : at + 8, :].reshape(size, LANES)
            high, low = split(value)
            c_both[0:size, shift * LANES : (shift + 1) * LANES] = high
            c_both[size : 2 * size, shift * LANES : (shift + 1) * LANES] = low
        both = c_both[...]
        at = (2 - window) * LANES
        term = mm(both, y_hi[:, at : at + 256])
        term = term[:size] + term[size:] + mm(both[:size], y_lo[:, at : at + 256])
        main = term if main is None else main + term
        term = mm(both, y_hi[:, 512:640])
        term = term[:size] + roll(term[:size], HALF) + term[size:]
        term = roll(term, 16 * (window - 2))
        edge = term if edge is None else edge + term

    copy_out.wait()
    lane = lane_iota(8)
    sub = lax.broadcasted_iota(jnp.int32, (8, LANES), 0)
    count_j = counts(xl * LANES, LANES, n_xl * LANES, lane)
    for x in range(2):
        for h in range(2):
            total = None
            for q in range(KI):
                s = q - HW
                rows = slice((x * KI + q) * 8, (x * KI + q) * 8 + 8)
                value = roll(main[rows, h * LANES : (h + 1) * LANES], s)
                if s != 0:
                    outer = roll(edge[rows, :], s - 8 - 16 * h)
                    value = jnp.where(lane < s if s > 0 else lane >= LANES + s, outer, value)
                total = value if total is None else total + value
            count_i = counts(inl * 16 + 8 * h, 16, n_inl * 16, sub)
            denoised_ref[x, 8 * h : 8 * h + 8, :] = total / (count_i * count_j)


def per_device(n_inl, n_xl, spectra, omega):
    vmem = pltpu.VMEM
    dma = pltpu.SemaphoreType.DMA
    here = pl.BlockSpec(memory_space=pltpu.VMEM)
    anywhere = pl.BlockSpec(memory_space=pl.ANY)
    limit = 24 * 1024 * 1024

    share = TROWS // n_inl
    inl_sems = [dma((n_inl,))] * 2
    xl_sems = [dma((n_xl,))] * 2
    results = pl.pallas_call(
        functools.partial(gather_kernel, n_inl, n_xl),
        out_shape=(
            jax.ShapeDtypeStruct((CH * 16, LANES), F32),
            jax.ShapeDtypeStruct((TROWS, LANES), F32),
            jax.ShapeDtypeStruct((HALF, LANES), F32),
            jax.ShapeDtypeStruct((8 * CH, 640), BF16),
            jax.ShapeDtypeStruct((8 * CH, 512), BF16),
        ),
        in_specs=[pl.BlockSpec(memory_space=pltpu.HBM)] * 2,
        out_specs=(here,) * 5,
        scratch_shapes=[
            vmem((3, 3, 2, 16, LANES), F32),
            vmem((2, HALF, KI * KI), F32),
            vmem((CH, TROWS), F32),
            vmem((8 * CH, KPAD), BF16),
            vmem((8 * CH, KPAD), BF16),
            vmem((KPAD, 640), BF16),
            vmem((KPAD, 640), BF16),
            vmem((KROWS + 8, 256), F32),
            vmem((TROWS, LANES), F32),
            vmem((32, LANES), F32),
            vmem((n_xl, 32, LANES), F32),
            vmem((32, LANES), F32),
            vmem((n_inl, 32, LANES), F32),
            vmem((HALF, LANES), F32),
            vmem((n_inl, share, LANES), F32),
            vmem((share, LANES), F32),
            vmem((n_xl, share, LANES), F32),
            vmem((share, LANES), F32),
            vmem((n_inl, share, LANES), F32),
            dma((8,)),
            dma((8,)),
            *inl_sems,
            *xl_sems,
            *inl_sems,
            *xl_sems,
            *inl_sems,
            dma,
            dma,
        ],
        compiler_params=pltpu.CompilerParams(
            collective_id=0, has_side_effects=True, vmem_limit_bytes=limit
        ),
    )(
        pltpu.with_memory_space_constraint(spectra[0], pltpu.HBM),
        pltpu.with_memory_space_constraint(omega.transpose(0, 2, 1), pltpu.HBM),
    )
    sketch, denoised = pl.pallas_call(
        functools.partial(spread_kernel, n_inl, n_xl),
        out_shape=(
            jax.ShapeDtypeStruct((CH * 16, LANES), F32),
            jax.ShapeDtypeStruct((2, 16, LANES), F32),
        ),
        in_specs=[anywhere] + [here] * 4,
        out_specs=(anywhere, here),
        scratch_shapes=[
            vmem((GROUPS, 32, LANES), F32),
            vmem((2 * GROUPS * 8, 8 * LANES), BF16),
            dma,
        ],
        compiler_params=pltpu.CompilerParams(vmem_limit_bytes=limit),
    )(*results)
    return sketch.reshape(1, CH, 16, LANES), denoised[None]


def solution(mesh):
    in_specs = (P("freq", None, "inl", "xl"), P())
    out_specs = (P("freq", None, "inl", "xl"), P("freq", None, "inl", "xl"))
    return jax.shard_map(
        functools.partial(per_device, mesh.shape["inl"], mesh.shape["xl"]),
        mesh=mesh,
        in_specs=in_specs,
        out_specs=out_specs,
        check_vma=False,
    )
```

```python
import functools

import jax
import jax.numpy as jnp
from jax import lax
from jax.experimental import pallas as pl
from jax.experimental.pallas import tpu as pltpu
from jax.sharding import PartitionSpec as P

MESH = pl.DeviceIdType.MESH
F32 = jnp.float32
BF16 = jnp.bfloat16
KI = 17
HW = 8
WIN = 24
GROUPS = 2 * KI
KROWS = GROUPS * WIN
KPAD = 896
TROWS = 384
LANES = 128
CH = 128
HALF = 64


def split(value):
    high = value.astype(BF16)
    return high, (value - high.astype(F32)).astype(BF16)


def mm(a, b):
    return jnp.dot(a, b, preferred_element_type=F32)


def mm_t(a, b):
    return lax.dot_general(a, b, (((1,), (1,)), ((), ())), preferred_element_type=F32)


def roll(value, amount, axis=1):
    size = value.shape[axis]
    amount = amount % size
    return value if amount == 0 else pltpu.roll(value, amount, axis)


def lane_iota(rows, lanes=LANES):
    return lax.broadcasted_iota(jnp.int32, (rows, lanes), 1)


def prepare_weights(omega_ref, taps_ref, band_hi, band_lo):
    taps_ref[:, 256:TROWS] = jnp.zeros((CH, TROWS - 256), F32)
    taps_ref[0:HALF, 0 : KI * KI] = omega_ref[0]
    taps_ref[HALF:CH, 0 : KI * KI] = omega_ref[1]
    tap_t = taps_ref[...]
    turned = jnp.concatenate([-tap_t[HALF:], tap_t[:HALF]], axis=0)
    col = lane_iota(1, KPAD)
    second = col >= KROWS // 2
    inner = jnp.where(second, col - KROWS // 2, col)
    q = (inner * 2731) >> 16
    r = inner - q * WIN
    tap = jnp.where((r < KI) & (col < KROWS), r * KI + q, -1)
    row = lax.broadcasted_iota(jnp.int32, (TROWS, KPAD), 0)
    pick_re = (row == jnp.where(second, -1, tap)).astype(F32).astype(BF16)
    pick_im = (row == jnp.where(second, tap, -1)).astype(F32).astype(BF16)
    re_hi, re_lo = split(tap_t)
    im_hi, im_lo = split(turned)
    wide_hi = mm(re_hi, pick_re) + mm(im_hi, pick_im)
    wide_lo = mm(re_lo, pick_re) + mm(im_lo, pick_im)
    for shift in range(8):
        band_hi[shift * CH : (shift + 1) * CH, :] = roll(wide_hi, shift).astype(BF16)
        band_lo[shift * CH : (shift + 1) * CH, :] = roll(wide_lo, shift).astype(BF16)


def shifted(left, centre, right, s, lane):
    if s == 0:
        return centre
    if s < 0:
        return jnp.where(lane < -s, roll(left, -s), roll(centre, -s))
    return jnp.where(lane >= LANES - s, roll(right, LANES - s), roll(centre, LANES - s))


def plane(block_ref, x, dc):
    return jnp.concatenate([block_ref[dr, dc, x] for dr in range(3)], axis=0)


def build_main(block_ref, s_hi, s_lo):
    lane = lane_iota(48)
    windows = []
    for x in range(2):
        left, centre, right = (plane(block_ref, x, dc) for dc in range(3))
        for q in range(KI):
            windows.append(shifted(left, centre, right, q - HW, lane))
    for k in range(KI):
        first, second = windows[2 * k], windows[2 * k + 1]
        for g in range(4):
            value = jnp.concatenate([first[8 * g : 8 * g + WIN], second[8 * g : 8 * g + WIN]], axis=0)
            high, low = split(value)
            s_hi[48 * k : 48 * k + 48, g * LANES : (g + 1) * LANES] = high
            s_lo[48 * k : 48 * k + 48, g * LANES : (g + 1) * LANES] = low


def build_side(block_ref, s_hi, s_lo):
    lane = lane_iota(48)
    strips = []
    for x in range(2):
        left, centre, right = (plane(block_ref, x, dc) for dc in range(3))
        for q in range(KI):
            inner = roll(centre, 16 - q)
            near = lane < 16 - q
            strip = jnp.where(
                lane < 8,
                jnp.where(near, roll(left, 16 - q), inner),
                jnp.where(near, inner, roll(right, 16 - q)),
            )
            strip = jnp.where(lane < 16, strip, 0.0)
            total = strip[0:WIN]
            for g in range(1, 4):
                total = total + roll(strip[8 * g : 8 * g + WIN], 16 * g)
            strips.append(total)
    for k in range(KI):
        high, low = split(jnp.concatenate([strips[2 * k], strips[2 * k + 1]], axis=0))
        s_hi[48 * k : 48 * k + 48, 512:640] = high
        s_lo[48 * k : 48 * k + 48, 512:640] = low


def invert(matrix):
    shape = (8, LANES)
    lane = lane_iota(8)
    pair = (lane & (HALF - 1)) >> 1
    sub = lax.broadcasted_iota(jnp.int32, shape, 0)
    turn = jnp.where(lane < HALF, -1.0, 1.0)
    tiles = [matrix[8 * v : 8 * v + 8] for v in range(HALF // 8)]

    def fill(value):
        return jnp.broadcast_to(value, shape)

    for k in range(0, HALF, 2):
        v, r = divmod(k, 8)
        row1, row2 = fill(tiles[v][r : r + 1, :]), fill(tiles[v][r + 1 : r + 2, :])
        a, d = fill(row1[:, k : k + 1]), fill(row2[:, k + 1 : k + 2])
        br, bi = fill(row1[:, k + 1 : k + 2]), fill(row1[:, HALF + k + 1 : HALF + k + 2])
        cut = pair == k // 2
        row1 = jnp.where(cut, jnp.where(lane == k, 1.0, 0.0), row1)
        row2 = jnp.where(cut, jnp.where(lane == k + 1, 1.0, 0.0), row2)
        turned1, turned2 = roll(row1, HALF) * turn, roll(row2, HALF) * turn
        p1 = 1.0 / a
        er, ei = br * p1, bi * p1
        p2 = 1.0 / (d - (br * er + bi * ei))
        new2 = p2 * (row2 - (er * row1 - ei * turned1))
        spun2 = p2 * (turned2 - (er * turned1 + ei * row1))
        new1 = p1 * row1 - (er * new2 + ei * spun2)
        spun1 = p1 * turned1 - (er * spun2 - ei * new2)
        after = []
        for w, tile in enumerate(tiles):
            first = fill(tile[:, k : k + 1]) * new1 + fill(tile[:, HALF + k : HALF + k + 1]) * spun1
            second = (
                fill(tile[:, k + 1 : k + 2]) * new2
                + fill(tile[:, HALF + k + 1 : HALF + k + 2]) * spun2
            )
            value = jnp.where(cut, 0.0, tile) - (first + second)
            if w == v:
                value = jnp.where(sub == r, new1, jnp.where(sub == r + 1, new2, value))
            after.append(value)
        tiles = after
    return jnp.concatenate(tiles, axis=0)


def counts(start, length, total, index):
    at = start + index
    return (jnp.minimum(at + HW, total - 1) - jnp.maximum(at - HW, 0) + 1).astype(F32)


def gather_kernel(
    n_inl,
    n_xl,
    spectra_ref,
    omega_hbm,
    sketch_ref,
    moments_ref,
    inverse_ref,
    y_hi,
    y_lo,
    block_ref,
    omega_ref,
    taps_ref,
    band_hi,
    band_lo,
    s_hi,
    s_lo,
    prod_ref,
    send_ref,
    gram_ref,
    gram_b,
    gram_part,
    gram_c,
    matrix_ref,
    recv_a,
    part_ref,
    recv_b,
    full_ref,
    recv_c,
    halo_send,
    halo_recv,
    a_send,
    a_recv,
    b_send,
    b_recv,
    c_send,
    c_recv,
    gb_send,
    gb_recv,
    gc_send,
    gc_recv,
    own_sem,
    omega_sem,
):
    own_copy = pltpu.make_async_copy(spectra_ref, block_ref.at[1, 1], own_sem)
    own_copy.start()
    omega_copy = pltpu.make_async_copy(omega_hbm, omega_ref, omega_sem)
    omega_copy.start()
    inl = lax.axis_index("inl")
    xl = lax.axis_index("xl")
    up, down = inl > 0, inl < n_inl - 1
    west, east = xl > 0, xl < n_xl - 1
    barrier = pltpu.get_barrier_semaphore()
    sides = [(-1, -1), (-1, 1), (1, -1), (1, 1), (-1, 0), (1, 0), (0, -1), (0, 1)]

    def exists(dr, dc):
        ok = None
        for step, low, high in ((dr, up, down), (dc, west, east)):
            if step != 0:
                one = low if step < 0 else high
                ok = one if ok is None else ok & one
        return ok

    def greet(axis, steps):
        me, count = (inl, n_inl) if axis == "inl" else (xl, n_xl)
        for k in steps:
            pl.semaphore_signal(
                barrier, inc=1, device_id={axis: lax.rem(me + k, count)}, device_id_type=MESH
            )

    greet("inl", sorted({1, n_inl - 1}))
    greet("xl", sorted({1, n_xl - 1}))
    expected = n_inl - 1 + n_xl - 1
    for dr, dc in sides:
        if dr != 0 and dc != 0:
            there = exists(dr, dc)
            expected = expected + there.astype(jnp.int32)

            @pl.when(there)
            def _(dr=dr, dc=dc):
                pl.semaphore_signal(
                    barrier, inc=1, device_id={"inl": inl + dr, "xl": xl + dc}, device_id_type=MESH
                )

    greet("inl", range(2, n_inl - 1))
    greet("xl", range(2, n_xl - 1))
    s_hi[KROWS:KPAD, :] = jnp.zeros((KPAD - KROWS, 640), BF16)
    s_lo[KROWS:KPAD, :] = jnp.zeros((KPAD - KROWS, 640), BF16)
    pl.semaphore_wait(barrier, expected)

    def halo(n, dr, dc):
        return pltpu.make_async_remote_copy(
            src_ref=spectra_ref,
            dst_ref=block_ref.at[1 - dr, 1 - dc],
            send_sem=halo_send.at[n],
            recv_sem=halo_recv.at[n],
            device_id={"inl": inl + dr, "xl": xl + dc},
            device_id_type=MESH,
        )

    for n, (dr, dc) in enumerate(sides):

        @pl.when(exists(dr, dc))
        def _(n=n, dr=dr, dc=dc):
            halo(n, dr, dc).start()

    for dr, dc in sides:

        @pl.when(jnp.logical_not(exists(dr, dc)))
        def _(dr=dr, dc=dc):
            block_ref[1 + dr, 1 + dc] = jnp.zeros((2, 16, LANES), F32)

    omega_copy.wait()
    prepare_weights(omega_ref, taps_ref, band_hi, band_lo)

    own_copy.wait()
    for n, (dr, dc) in enumerate(sides):

        @pl.when(exists(dr, dc))
        def _(n=n, dr=dr, dc=dc):
            halo(n, dr, dc).wait_send()

        @pl.when(exists(-dr, -dc))
        def _(n=n, dr=dr, dc=dc):
            halo(n, dr, dc).wait_recv()

    def sketch_rows(shift, at, width):
        rows = slice(shift * CH, (shift + 1) * CH)
        left_hi = band_hi[rows, :]
        right = s_hi[:, at : at + width]
        return mm(left_hi, right) + mm(band_lo[rows, :], right) + mm(left_hi, s_lo[:, at : at + width])

    def piece(at):
        share = TROWS // n_inl
        return pl.ds(pl.multiple_of(at * share, 8), share)

    def exchange(axis, source, slots, sems):
        me, count = (inl, n_inl) if axis == "inl" else (xl, n_xl)
        send, recv = sems
        pieces = source.shape[0] != slots.shape[1]

        def copy(k):
            peer = lax.rem(me + k, count)
            return pltpu.make_async_remote_copy(
                src_ref=source.at[piece(peer)] if pieces else source,
                dst_ref=slots.at[me],
                send_sem=send.at[k],
                recv_sem=recv.at[k],
                device_id={axis: peer},
                device_id_type=MESH,
            )

        def hops(k):
            if axis == "xl":
                return min(k, count - k)
            return min(k // 4, count // 4 - k // 4) + min(k % 4, 4 - k % 4)

        far_first = sorted(range(1, count), key=hops, reverse=True)

        def start():
            for k in far_first:
                copy(k).start()
            slots[me] = source[piece(me), :] if pieces else source[...]

        def wait():
            for k in range(1, count):
                copy(k).wait()

        return start, wait

    def summed(slots):
        values = [slots[k] for k in range(slots.shape[0])]
        while len(values) > 1:
            values = [a + b for a, b in zip(values[::2], values[1::2])]
        return values[0]

    gram_xl = exchange("xl", gram_ref, gram_b, (gb_send, gb_recv))
    gram_inl = exchange("inl", gram_part, gram_c, (gc_send, gc_recv))
    scatter_inl = exchange("inl", send_ref, recv_a, (a_send, a_recv))
    across_xl = exchange("xl", part_ref, recv_b, (b_send, b_recv))
    gather_inl = exchange("inl", full_ref, recv_c, (c_send, c_recv))

    stage = pl.loop(0, 1 + jnp.minimum(inl, 0))

    @stage
    def _(_once):
        build_main(block_ref, s_hi, s_lo)
        sums = None
        for shift in range(8):
            value = sketch_rows(shift, LANES, 2 * LANES)
            for half in range(2):
                sketch_ref[pl.ds(8 * half + shift, CH, stride=16), :] = value[
                    :, half * LANES : (half + 1) * LANES
                ]
            high, low = split(value)
            y_hi[shift * CH : (shift + 1) * CH, 128:384] = high
            y_lo[shift * CH : (shift + 1) * CH, 128:384] = low
            term = mm_t(jnp.concatenate([high, low], axis=0), high)
            sums = term if sums is None else sums + term
        sign = jnp.where(lane_iota(1) < HALF, 1.0, -1.0)
        products = sums[:CH] + (sums[CH:] + sums[CH:].T)
        gram = products[:HALF] + roll(products[HALF:], HALF) * sign
        lane = lane_iota(HALF)
        sub = lax.broadcasted_iota(jnp.int32, (HALF, LANES), 0)
        gram = jnp.where(sub >= lane, gram, roll(gram, HALF))
        gram_ref[...] = jnp.where(lane[:32] < HALF, gram[:32], roll(gram[32:], HALF))
        gram_xl[0]()

    @stage
    def _(_once):
        main_hi, main_lo = s_hi[0:KROWS, 128:384], s_lo[0:KROWS, 128:384]
        prod_ref[KROWS : KROWS + 8, :] = jnp.zeros((8, 256), F32)
        total = None
        for pair in range(4):
            rows = slice(pair * 256, (pair + 1) * 256)
            own_hi = y_hi[rows, 128:384]
            prod_ref[0:KROWS, :] = (
                mm_t(main_hi, own_hi) + mm_t(main_lo, own_hi) + mm_t(main_hi, y_lo[rows, 128:384])
            )
            for k in range(2):
                term = prod_ref[2 * pair + k : 2 * pair + k + KROWS, k * LANES : (k + 1) * LANES]
                total = term if total is None else total + term
        prod_ref[0:KROWS, 0:LANES] = total
        first = prod_ref[0 : KROWS // 2, 0:LANES]
        second = prod_ref[KROWS // 2 : KROWS, 0:LANES]
        sign = jnp.where(lane_iota(1) < HALF, 1.0, -1.0)
        moments = roll(second, HALF) + first * sign
        for q in range(KI):
            send_ref[q * 16 : q * 16 + 16, :] = moments[q * WIN : q * WIN + 16]
            send_ref[272 + q : 273 + q, :] = moments[q * WIN + 16 : q * WIN + 17]
        send_ref[289:TROWS, :] = jnp.zeros((TROWS - 289, LANES), F32)
        scatter_inl[0]()

    def outer_rows(shifts):
        side_lane = lane_iota(1)
        keep_up = up.astype(F32)
        keep_down = down.astype(F32)
        keep_side = jnp.where(side_lane % 16 < 8, west.astype(F32), east.astype(F32)) * jnp.where(
            side_lane < 16, keep_up, jnp.where((side_lane >= 48) & (side_lane < 64), keep_down, 1.0)
        )
        keep = jnp.concatenate([jnp.full((1, LANES), keep_down), keep_side], axis=1)
        for shift in shifts:
            rows = slice(shift * CH, (shift + 1) * CH)
            high, low = split(sketch_rows(shift, 0, LANES) * keep_up)
            y_hi[rows, 0:128] = high
            y_lo[rows, 0:128] = low
            high, low = split(sketch_rows(shift, 384, 256) * keep)
            y_hi[rows, 384:512] = high[:, :LANES]
            y_lo[rows, 384:512] = low[:, :LANES]
            rest = roll(low[:, LANES:].astype(F32), HALF)
            y_hi[rows, 512:640] = jnp.where(side_lane < HALF, high[:, LANES:].astype(F32), rest).astype(BF16)

    @stage
    def _(_once):
        build_side(block_ref, s_hi, s_lo)
        outer_rows(range(4))

    @stage
    def _(_once):
        gram_xl[1]()
        gram_part[...] = summed(gram_b)
        gram_inl[0]()

    @stage
    def _(_once):
        scatter_inl[1]()
        part_ref[...] = summed(recv_a)
        across_xl[0]()

    @stage
    def _(_once):
        outer_rows(range(4, 8))

    @stage
    def _(_once):
        gram_inl[1]()
        packed = summed(gram_c)
        packed = jnp.concatenate([packed, roll(packed, HALF)], axis=0)
        flipped = jnp.concatenate([packed, jnp.zeros_like(packed)], axis=0).T[:HALF]
        lane = lane_iota(HALF)
        sub = lax.broadcasted_iota(jnp.int32, (HALF, LANES), 0)
        real = jnp.where(sub >= lane, packed, flipped)
        imag = jnp.where(sub < lane, packed, jnp.where(sub > lane, -flipped, 0.0))
        matrix_ref[...] = jnp.where(lane < HALF, real, roll(imag, HALF))

    @stage
    def _(_once):
        across_xl[1]()
        full_ref[...] = summed(recv_b)
        gather_inl[0]()

    @stage
    def _(_once):
        inverse_ref[...] = invert(matrix_ref[...])

    @stage
    def _(_once):
        gather_inl[1]()
        moments_ref[...] = recv_c[...].reshape(TROWS, LANES)


def spread_kernel(
    n_inl,
    n_xl,
    sketch_ref,
    moments_ref,
    inverse_ref,
    y_hi,
    y_lo,
    sketch_out,
    denoised_ref,
    spread_ref,
    c_both,
    out_sem,
):
    inl = lax.axis_index("inl")
    xl = lax.axis_index("xl")
    copy_out = pltpu.make_async_copy(sketch_ref, sketch_out, out_sem)
    copy_out.start()
    sign = jnp.where(lane_iota(1) < HALF, 1.0, -1.0)
    inverse = inverse_ref[...]
    mixing = jnp.concatenate([inverse * sign, roll(inverse, HALF)], axis=0)
    mixing_hi, mixing_lo = split(mixing)
    high, low = split(moments_ref[...])
    coeffs = mm(high, mixing_hi) + mm(low, mixing_hi) + mm(high, mixing_lo)

    spread_ref[:, 0:8, :] = jnp.zeros((GROUPS, 8, LANES), F32)
    spread_ref[:, 24:32, :] = jnp.zeros((GROUPS, 8, LANES), F32)
    for x, value in enumerate((coeffs * sign, roll(coeffs, HALF))):
        for q in range(KI):
            spread_ref[x * KI + q, 8:24, :] = value[q * 16 : q * 16 + 16]
            spread_ref[x * KI + q, 24:25, :] = value[272 + q : 273 + q]

    size = GROUPS * 8
    for window in range(3):
        for shift in range(8):
            at = 8 + 8 * window - shift
            value = spread_ref[:, at : at + 8, :].reshape(size, LANES)
            high, low = split(value)
            lanes = slice((8 * window + shift) * LANES, (8 * window + shift + 1) * LANES)
            c_both[0:size, lanes] = high
            c_both[size : 2 * size, lanes] = low

    def stacked(ref):
        return jnp.concatenate([ref[:, at : at + 256] for at in (2 * LANES, LANES, 0)], axis=0)

    main = mm(c_both[...], stacked(y_hi))
    main = main[:size] + main[size:] + mm(c_both[0:size, :], stacked(y_lo))
    edge = None
    for window in range(3):
        term = mm(c_both[:, 1024 * window : 1024 * (window + 1)], y_hi[:, 512:640])
        term = term[:size] + roll(term[:size], HALF) + term[size:]
        term = roll(term, 16 * (window - 2))
        edge = term if edge is None else edge + term

    copy_out.wait()
    lane = lane_iota(8)
    sub = lax.broadcasted_iota(jnp.int32, (8, LANES), 0)
    count_j = counts(xl * LANES, LANES, n_xl * LANES, lane)
    for x in range(2):
        for h in range(2):
            total = None
            for q in range(KI):
                s = q - HW
                rows = slice((x * KI + q) * 8, (x * KI + q) * 8 + 8)
                value = roll(main[rows, h * LANES : (h + 1) * LANES], s)
                if s != 0:
                    outer = roll(edge[rows, :], s - 8 - 16 * h)
                    value = jnp.where(lane < s if s > 0 else lane >= LANES + s, outer, value)
                total = value if total is None else total + value
            count_i = counts(inl * 16 + 8 * h, 16, n_inl * 16, sub)
            denoised_ref[x, 8 * h : 8 * h + 8, :] = total / (count_i * count_j)


def per_device(n_inl, n_xl, spectra, omega):
    vmem = pltpu.VMEM
    dma = pltpu.SemaphoreType.DMA
    here = pl.BlockSpec(memory_space=pltpu.VMEM)
    anywhere = pl.BlockSpec(memory_space=pl.ANY)
    limit = 24 * 1024 * 1024

    share = TROWS // n_inl
    inl_sems = [dma((n_inl,))] * 2
    xl_sems = [dma((n_xl,))] * 2
    results = pl.pallas_call(
        functools.partial(gather_kernel, n_inl, n_xl),
        out_shape=(
            jax.ShapeDtypeStruct((CH * 16, LANES), F32),
            jax.ShapeDtypeStruct((TROWS, LANES), F32),
            jax.ShapeDtypeStruct((HALF, LANES), F32),
            jax.ShapeDtypeStruct((8 * CH, 640), BF16),
            jax.ShapeDtypeStruct((8 * CH, 512), BF16),
        ),
        in_specs=[pl.BlockSpec(memory_space=pltpu.HBM)] * 2,
        out_specs=(here,) * 5,
        scratch_shapes=[
            vmem((3, 3, 2, 16, LANES), F32),
            vmem((2, HALF, KI * KI), F32),
            vmem((CH, TROWS), F32),
            vmem((8 * CH, KPAD), BF16),
            vmem((8 * CH, KPAD), BF16),
            vmem((KPAD, 640), BF16),
            vmem((KPAD, 640), BF16),
            vmem((KROWS + 8, 256), F32),
            vmem((TROWS, LANES), F32),
            vmem((32, LANES), F32),
            vmem((n_xl, 32, LANES), F32),
            vmem((32, LANES), F32),
            vmem((n_inl, 32, LANES), F32),
            vmem((HALF, LANES), F32),
            vmem((n_inl, share, LANES), F32),
            vmem((share, LANES), F32),
            vmem((n_xl, share, LANES), F32),
            vmem((share, LANES), F32),
            vmem((n_inl, share, LANES), F32),
            dma((8,)),
            dma((8,)),
            *inl_sems,
            *xl_sems,
            *inl_sems,
            *xl_sems,
            *inl_sems,
            dma,
            dma,
        ],
        compiler_params=pltpu.CompilerParams(
            collective_id=0, has_side_effects=True, vmem_limit_bytes=limit
        ),
    )(
        pltpu.with_memory_space_constraint(spectra[0], pltpu.HBM),
        pltpu.with_memory_space_constraint(omega.transpose(0, 2, 1), pltpu.HBM),
    )
    sketch, denoised = pl.pallas_call(
        functools.partial(spread_kernel, n_inl, n_xl),
        out_shape=(
            jax.ShapeDtypeStruct((CH * 16, LANES), F32),
            jax.ShapeDtypeStruct((2, 16, LANES), F32),
        ),
        in_specs=[anywhere] + [here] * 4,
        out_specs=(anywhere, here),
        scratch_shapes=[
            vmem((GROUPS, 32, LANES), F32),
            vmem((2 * GROUPS * 8, 24 * LANES), BF16),
            dma,
        ],
        compiler_params=pltpu.CompilerParams(vmem_limit_bytes=limit),
    )(*results)
    return sketch.reshape(1, CH, 16, LANES), denoised[None]


def solution(mesh):
    in_specs = (P("freq", None, "inl", "xl"), P())
    out_specs = (P("freq", None, "inl", "xl"), P("freq", None, "inl", "xl"))
    return jax.shard_map(
        functools.partial(per_device, mesh.shape["inl"], mesh.shape["xl"]),
        mesh=mesh,
        in_specs=in_specs,
        out_specs=out_specs,
        check_vma=False,
    )
```
